32 devices in a mesh: leaf: 16 (over z, y, x), vec: 2 (over core).
Axes of the slice: x: 2, y: 2, z: 4, core: 2. Of those that a mesh axis runs over, the one named last changes fastest.
Arguments:
- points: bfloat16 [3, 131072], P(None, 'leaf'), may hold values from -4 to 4
- vectors: bfloat16 [16, 131072], P('vec', 'leaf'), may hold values from -6 to 6
- leaf_order: int32 [16, 8192], P('leaf'), may hold values from 0 to 8191, each once within a row
- leaf_bases: bfloat16 [256, 64, 512], P('leaf'), may hold values from -0.25 to 0.25
- transfers: bfloat16 [480, 64, 64], P('leaf'), may hold values from -0.5 to 0.5
- coupling_blocks: bfloat16 [4096, 64, 64], P('leaf'), may hold values from -0.75 to 0.75
- block_source: int32 [4096], P('leaf'), may hold values from 0 to 30, as said below
- block_owner: int32 [4096, 1], P('leaf'), may hold values from 0 to 15; in each aligned block of 256 rows (0 to 255, 256 to 511, ...) at most 32 rows name the same one
- block_target: int32 [4096], P('leaf'), may hold values from 0 to 30, as said below
- up_transfer: bfloat16 [30, 64, 64], replicated, may hold values from -0.5 to 0.5
- up_coupling: bfloat16 [30, 64, 64], replicated, as said below
Outputs:
- product: bfloat16 [16, 131072], P('vec', 'leaf')
The draws below stay inside these ranges and needn't reach their ends.
Inputs may be any that keep to these rules, and one draw needn't show every extreme that they name: `leaf_order`: within each row, each point of the device once. `block_source`: A cluster of the subtree of the device that stores the block, numbered leaves first and level by level up to the root. `block_target`: A cluster of the subtree of the device block_owner names, in the same numbering, on the same level as the block's source cluster. `block_owner`: of the 256 blocks stored on one device, at most 32 name the same device, and exactly 32 name some device; every device is named by some block. `up_coupling`: coupling matrices of sibling clusters of the upper tree, finite.
All inputs are finite; a program needn't handle non-finite values.
Results may differ from the reference program's by a relative error of at most 0.0065.
Values may be sent and summed in bfloat16 or wider, within the bound.
A program may use at most 128 MiB of HBM per device.

```python
import math
import jax
import jax.numpy as jnp
import numpy as np
from jax import lax

K = 64
LEAF = 512
NV = 16
NEAR = 2
LEAF_DEV = 16
LEAVES = 256
NPTS = 131072
NCL = 31
NTR = 30
NBLK = 256
CAP = 32
UP_NODES = 30
N_LEAF = 16


def level_pairs(key):
    count = N_LEAF * NBLK
    depth = LEAF_DEV.bit_length() - 1
    level = jax.random.randint(jax.random.fold_in(key, 11), (count,), 0, depth + 1, jnp.int32)
    level_width = jnp.right_shift(jnp.int32(LEAF_DEV), level)
    level_start = 2 * LEAF_DEV - 2 * level_width
    source_pick = jax.random.randint(jax.random.fold_in(key, 12), (count,), 0, LEAF_DEV, jnp.int32)
    target_pick = jax.random.randint(jax.random.fold_in(key, 13), (count,), 0, LEAF_DEV, jnp.int32)
    sources = level_start + source_pick % level_width
    targets = level_start + target_pick % level_width
    return (sources.astype(jnp.int32), targets.astype(jnp.int32))


def draw_block_source(key, part):
    return level_pairs(key)[0]


def draw_block_target(key, part):
    return level_pairs(key)[1]


def draw_up_coupling(key, part):
    node_ids = jnp.arange(UP_NODES, dtype=jnp.int32)
    whole_count = UP_NODES + 2
    tier = jnp.zeros((UP_NODES,), jnp.float32)
    for shift_no in range(1, 24):
        tier = tier + (node_ids >= whole_count - (whole_count >> shift_no)).astype(jnp.float32)
    local_levels = LEAF_DEV.bit_length() - 1
    scales = jnp.power(2.0, (tier + local_levels) / 2.0) / math.sqrt(K)
    base_draw = jnp.clip(jax.random.normal(key, (UP_NODES, K, K), jnp.float32), -4.0, 4.0)
    return (base_draw * scales[:, None, None]).astype(jnp.bfloat16)


def level_of(key, dims, shards, smallest, largest):
    factor_of = 1.0
    for position, blocks in shards:
        heights = jax.random.uniform(jax.random.fold_in(jax.random.fold_in(key, 6), position), (blocks,), jnp.float32, smallest / len(shards), largest / len(shards))
        factor_of = factor_of * jnp.repeat(jnp.exp(heights), dims[position] // blocks).reshape((-1,) + (1,) * (len(dims) - 1 - position))
    return factor_of


def assign_block(stream_key, own, number, rows, amount, top, most, skew):
    ranking = jax.random.permutation(stream_key, amount)
    packed, usual = shares(amount, rows * top, most, skew, True), shares(amount, rows * top, most, skew, False)
    places = jnp.arange(amount)

    def named(lengths, turn):
        used = int((lengths > 0).sum())
        fixed = max(1, used // 4)
        shifted = fixed + (places - fixed + turn * (used - fixed)) % max(1, amount - fixed)
        return jnp.zeros((amount,), jnp.int32).at[ranking[jnp.where(places < fixed, places, shifted)]].set(jnp.asarray(lengths, jnp.int32))

    lengths = jnp.where(number % 4 == 0, named(packed, number // 4), named(usual, number - number // 4 - 1))
    mixed = jax.random.permutation(jax.random.fold_in(own, 3), amount)
    source_of, sink = mixed[0:amount // 2 * 2:2], mixed[1:amount // 2 * 2:2]
    margin = jnp.minimum(lengths[source_of] - 1, most - lengths[sink]) // 2
    margin = jnp.where((source_of == ranking[0]) | (sink == ranking[0]) | (lengths[sink] == 0), 0, jnp.maximum(margin, 0))
    shifted = jax.random.randint(jax.random.fold_in(own, 4), (amount // 2,), 0, 1 << 20) % (margin + 1)
    lengths = lengths.at[source_of].add(-shifted).at[sink].add(shifted)
    members = jnp.searchsorted(jnp.cumsum(lengths), jnp.arange(rows * top), side="right").astype(jnp.int32)
    listing = members.reshape(top, rows).T
    listing = listing[jax.random.permutation(jax.random.fold_in(own, 1), rows)]
    turn = jax.random.randint(jax.random.fold_in(own, 2), (rows, 1), 0, top)
    return jnp.take_along_axis(listing, (jnp.arange(top)[None, :] + turn) % top, axis=1)


def shares(number_of, total, bound, slope, full):
    loads = [(1 << 20) // math.isqrt(rank ** slope) + 1 for rank in range(1, number_of + 1)]
    largest = bound if full else min(bound, max(-(-total // number_of), total * loads[0] // sum(loads)))
    least = 1 if total - largest >= number_of - 1 else 0
    holding, rest = [largest] + [least] * (number_of - 1), total - largest - least * (number_of - 1)
    while rest > 0:
        movable = [i for i in range(1, number_of) if holding[i] < largest] or [i for i in range(1, number_of) if holding[i] < bound]
        pool, remaining = sum([loads[i] for i in movable]), rest
        for i in movable:
            more = min(bound - holding[i], max(1, remaining * loads[i] // pool), rest)
            holding[i] = holding[i] + more
            rest = rest - more
    return np.array(holding)


def bell_draw(own_key, shape, deviation, limit, shards=(), kind=jnp.bfloat16):
    result = deviation * jax.random.normal(own_key, shape, jnp.float32)
    if shards:
        result = result * level_of(own_key, shape, shards, -0.22, 0.18)
    return jnp.clip(result, -limit, limit).astype(kind)


def setup_inputs(seed: int = 0) -> dict:
    seeds = jax.random.split(jax.random.key(seed), 12)
    points = bell_draw(seeds[0], (3, NPTS), 1.0, 4.0, ((1, 16),))
    vectors = bell_draw(seeds[1], (NV, NPTS), 1.0, 6.0, ((0, 2), (1, 16)))
    leaf_order = jax.vmap(lambda own: jax.random.permutation(own, LEAF_DEV * LEAF))(jax.random.split(seeds[2], N_LEAF)).reshape((N_LEAF, LEAF_DEV * LEAF)).astype(jnp.int32)
    leaf_bases = bell_draw(seeds[3], (LEAVES, K, LEAF), LEAF ** -0.5, 0.25, ((0, 16),))
    transfers = bell_draw(seeds[4], (N_LEAF * NTR, K, K), (2 * K) ** -0.5, 0.5, ((0, 16),))
    coupling_blocks = bell_draw(seeds[5], (N_LEAF * NBLK, K, K), K ** -0.5, 0.75, ((0, 16),))
    block_source = draw_block_source(jax.random.fold_in(seeds[11], 71), 0)
    block_owner_keys = jax.random.split(jax.random.fold_in(seeds[7], 1), (N_LEAF * NBLK) // NBLK)
    block_owner_turns = jax.random.permutation(jax.random.fold_in(seeds[7], 3), (N_LEAF * NBLK) // NBLK)
    block_owner = jax.vmap(lambda own, number: assign_block(jax.random.fold_in(seeds[7], 2), own, number, NBLK, N_LEAF, 1, CAP, 2))(block_owner_keys, block_owner_turns).reshape((N_LEAF * NBLK, 1))
    block_target = draw_block_target(jax.random.fold_in(seeds[11], 71), 0)
    up_transfer = bell_draw(seeds[9], (UP_NODES, K, K), (2 * K) ** -0.5, 0.5)
    up_coupling = draw_up_coupling(jax.random.fold_in(seeds[11], 71), 0)
    return {"points": points, "vectors": vectors, "leaf_order": leaf_order, "leaf_bases": leaf_bases, "transfers": transfers, "coupling_blocks": coupling_blocks, "block_source": block_source, "block_owner": block_owner, "block_target": block_target, "up_transfer": up_transfer, "up_coupling": up_coupling}


near_scale = 8.0
smooth_sq = 0.0025
highest = lax.Precision.HIGHEST

def kernel_block(sources, targets):
    source_f = sources.astype(jnp.float32)
    target_f = targets.astype(jnp.float32)
    distance = (source_f[0][:, None] - target_f[0][None, :]) ** 2
    distance = distance + (source_f[1][:, None] - target_f[1][None, :]) ** 2
    distance = distance + (source_f[2][:, None] - target_f[2][None, :]) ** 2
    return lax.rsqrt(distance + smooth_sq).astype(jnp.bfloat16)

def near_block(padded, first_leaf, number, leaf_len):
    reach = NEAR * leaf_len
    window_len = (2 * NEAR + 1) * leaf_len

    def one_leaf(leaf_no):
        start_col = (first_leaf + leaf_no) * leaf_len
        targets = lax.dynamic_slice_in_dim(padded, start_col + reach, leaf_len, 1)
        window = lax.dynamic_slice_in_dim(padded, start_col, window_len, 1)
        kernel = kernel_block(window[:3], targets[:3])
        return jnp.dot(window[3:], kernel, preferred_element_type=jnp.float32) * (near_scale / leaf_len)
    per_leaf = lax.map(one_leaf, jnp.arange(number, dtype=jnp.int32))
    return jnp.transpose(per_leaf, (1, 0, 2)).reshape(per_leaf.shape[1], number * leaf_len)

def climb(children, matrices):
    moved_rows = jnp.einsum('...jvk,...jkp->...jvp', children, matrices.astype(jnp.float32), precision=highest)
    return moved_rows[..., 0::2, :, :] + moved_rows[..., 1::2, :, :]

def descend(parent, matrices):
    spread = jnp.repeat(parent, 2, axis=-3)
    return jnp.einsum('...jvp,...jkp->...jvk', spread, matrices.astype(jnp.float32), precision=highest)

def upper_tree(roots, up_transfer, up_coupling):
    current = roots
    gain_list = []
    offset = 0
    number = roots.shape[0]
    while number > 1:
        matrices = up_transfer[offset:offset + number].astype(jnp.float32)
        partner = current.reshape(number // 2, 2, current.shape[1], current.shape[2])[:, ::-1].reshape(current.shape)
        gain_term = jnp.einsum('jvk,jkp->jvp', partner, up_coupling[offset:offset + number].astype(jnp.float32), precision=highest)
        gain_list.append((matrices, gain_term))
        current = climb(current, matrices)
        offset += number
        number //= 2
    top_down = jnp.zeros_like(current)
    for matrices, gain_term in reversed(gain_list):
        top_down = descend(top_down, matrices) + gain_term
    return top_down

def reorder(array, permute):
    per_dev = LEAF_DEV * LEAF
    row_count = array.shape[0]
    blocked = array.reshape(row_count, N_LEAF, per_dev)
    picks = jnp.broadcast_to(permute[None], (row_count, N_LEAF, per_dev))
    return jnp.take_along_axis(blocked, picks, axis=2).reshape(row_count, NPTS)

def reference(points, vectors, leaf_order, leaf_bases, transfers, coupling_blocks, block_source, block_owner, block_target, up_transfer, up_coupling):
    per_dev = LEAF_DEV * LEAF
    points_tree = reorder(points, leaf_order)
    vectors_tree = reorder(vectors, leaf_order)
    reach = NEAR * LEAF
    joined = jnp.concatenate([points_tree, vectors_tree], axis=0)
    padded = jnp.pad(joined, ((0, 0), (reach, reach)))
    near_part = near_block(padded, 0, LEAVES, LEAF)
    shaped = vectors_tree.reshape(NV, LEAVES, LEAF).astype(jnp.float32)
    leaf_coeff = jnp.einsum('vlp,lkp->lvk', shaped, leaf_bases.astype(jnp.float32), precision=highest)
    leaf_coeff = leaf_coeff.reshape(N_LEAF, LEAF_DEV, NV, K)
    trans_all = transfers.reshape(N_LEAF, NTR, K, K)
    levels = [leaf_coeff]
    offset = 0
    number = LEAF_DEV
    while number > 1:
        levels.append(climb(levels[-1], trans_all[:, offset:offset + number]))
        offset += number
        number //= 2
    all_coeff = jnp.concatenate(levels, axis=1)
    top_down = upper_tree(all_coeff[:, NCL - 1], up_transfer, up_coupling)
    coeff_bf = all_coeff.astype(jnp.bfloat16)
    owner_dev = jnp.arange(N_LEAF * NBLK, dtype=jnp.int32) // NBLK
    picked = coeff_bf[owner_dev, block_source].astype(jnp.float32)
    products = jnp.einsum('bvk,bkp->bvp', picked, coupling_blocks.astype(jnp.float32), precision=highest)
    flat_target = block_owner[:, 0] * NCL + block_target
    coupled = jax.ops.segment_sum(products, flat_target, num_segments=N_LEAF * NCL).reshape(N_LEAF, NCL, NV, K)
    current = (top_down + coupled[:, NCL - 1])[:, None]
    number = 1
    while number < LEAF_DEV:
        number *= 2
        offset = 2 * LEAF_DEV - 2 * number
        current = descend(current, trans_all[:, offset:offset + number]) + coupled[:, offset:offset + number]
    down_leaf = lax.optimization_barrier(current.astype(jnp.bfloat16)).astype(jnp.float32)
    bases_f = leaf_bases.reshape(N_LEAF, LEAF_DEV, K, LEAF).astype(jnp.float32)
    far_part = jnp.einsum('nlvk,nlkp->vnlp', down_leaf, bases_f, precision=highest).reshape(NV, NPTS)
    tree_out = (far_part + near_part).astype(jnp.bfloat16)
    row_ids = jnp.arange(N_LEAF, dtype=jnp.int32)[:, None]
    positions = jnp.broadcast_to(jnp.arange(per_dev, dtype=jnp.int32)[None], (N_LEAF, per_dev))
    inverse = jnp.zeros((N_LEAF, per_dev), jnp.int32).at[row_ids, leaf_order].set(positions)
    return reorder(tree_out, inverse)
```

```python
import functools

import jax
import jax.numpy as jnp
from jax import lax
from jax.experimental import pallas as pl
from jax.experimental.pallas import tpu as pltpu
from jax.sharding import PartitionSpec as P

NEAR = 2
WIDTH = 256
ROWS = 16
SLOTS = 32
near_scale = 8.0
smooth_sq = 0.0025
f32, bf16, i32 = jnp.float32, jnp.bfloat16, jnp.int32


def contract(left, right, dim_left, dim_right):
    return lax.dot_general(
        left, right, (((dim_left,), (dim_right,)), ((), ())), preferred_element_type=f32
    )


def nn(left, right):
    return contract(left, right, 1, 0)


def nt(left, right):
    return contract(left, right, 1, 1)


def tn(left, right):
    return contract(left, right, 0, 0)


def two_parts(value):
    high = value.astype(bf16).astype(f32)
    return jnp.concatenate([high, value - high], axis=0).astype(bf16)


def wide(product, value, matrix):
    count = value.shape[0]
    both = product(two_parts(value), matrix)
    return both[:count] + both[count:]


def one_hot(rows, index):
    ids = lax.broadcasted_iota(i32, (rows, index.shape[1]), 0)
    return jnp.where(ids == index, 1.0, 0.0).astype(bf16)


def twice(value):
    return jnp.concatenate([value, value], axis=1)


def leaf_columns(leaf, leaf_len):
    return pl.ds(pl.multiple_of(leaf * leaf_len, leaf_len), leaf_len)


def to_tree(vec_ref, pts_ref, perm_ref, bases_ref, tree_ref, tree_base, both, stack, coeff):
    local, cols = vec_ref.shape
    leaf_dev, rank, leaf_len = bases_ref.shape
    groups = cols // WIDTH
    both[...] = jnp.zeros_like(both)
    both[0:local] = vec_ref[...].astype(f32)
    both[8:11] = pts_ref[...].astype(f32)
    for group in range(groups):
        stack[group * ROWS : (group + 1) * ROWS, :] = both[
            :, group * WIDTH : (group + 1) * WIDTH
        ].astype(bf16)

    def one_leaf(leaf, carry):
        perm = perm_ref[:, leaf_columns(leaf, leaf_len)]
        high = perm // WIDTH
        picked = nn(stack[...], one_hot(WIDTH, perm % WIDTH))
        total = jnp.where(high == 0, picked[:ROWS], 0.0)
        for group in range(1, groups):
            total = total + jnp.where(
                high == group, picked[group * ROWS : (group + 1) * ROWS], 0.0
            )
        tree = total.astype(bf16)
        tree_ref[:, leaf_columns(leaf + tree_base, leaf_len)] = tree
        own = nt(tree, bases_ref[leaf])[:local]
        coeff[pl.ds(pl.multiple_of(leaf * 8, 8), 8), :] = twice(own)
        return carry

    lax.fori_loop(0, leaf_dev, one_leaf, 0)


def climb(leaf_dev, rank, trans_ref, coeff):
    clusters = 2 * leaf_dev - 1
    coeff[clusters * 8 :, :] = jnp.zeros((coeff.shape[0] - clusters * 8, 2 * rank), f32)
    offset, number = 0, leaf_dev
    while number > 1:
        for parent in range(number // 2):
            total = 0.0
            for child in (offset + 2 * parent, offset + 2 * parent + 1):
                value = coeff[child * 8 : child * 8 + 8, :rank]
                total = total + wide(nn, value, trans_ref[child])
            place = (offset + number + parent) * 8
            coeff[place : place + 8, :] = twice(total)
        offset += number
        number //= 2


def couple(peers, blocks_ref, src_ref, dest_ref, coeff, picked, made, send_ref):
    blocks, rank, _ = blocks_ref.shape
    clusters = coeff.shape[0] // 8
    hot = one_hot(clusters, src_ref[...])
    for vec in range(8):
        values = coeff[pl.ds(vec, clusters, stride=8), :].astype(bf16)
        picked[pl.ds(vec, blocks, stride=8), :] = tn(hot, values)
    quad = 4 * rank
    row = lax.broadcasted_iota(i32, (32, quad), 0) // 8
    lane = lax.broadcasted_iota(i32, (32, quad), 1) // rank
    mine = row == lane

    def four(step, carry):
        rows = pl.ds(pl.multiple_of(step * 32, 32), 32)
        value = jnp.where(mine, twice(picked[rows, :]), 0.0).astype(bf16)
        matrix = blocks_ref[pl.ds(step * 4, 4)].reshape(quad, rank)
        made[rows, :] = twice(nn(value, matrix))
        return carry

    lax.fori_loop(0, blocks // 4, four, 0, unroll=8)
    pairs = []
    for vec in range(0, 8, 2):
        first = made[pl.ds(vec, blocks, stride=8), :][:, :rank]
        second = made[pl.ds(vec + 1, blocks, stride=8), :][:, :rank]
        pairs.append(jnp.concatenate([first, second], axis=1))
    all_made = jnp.concatenate(pairs, axis=1).astype(bf16)
    dest = dest_ref[...]
    step_rows = 16 * SLOTS

    def some(step, carry):
        start = pl.multiple_of(step * step_rows, step_rows)
        send_ref[pl.ds(start, step_rows), :] = nn(
            one_hot(step_rows, dest - start), all_made
        ).astype(bf16)
        return carry

    lax.fori_loop(0, peers * SLOTS // step_rows, some, 0)


def spread_kernel(
    peers, vec_ref, pts_ref, perm_ref, bases_ref, trans_ref, blocks_ref, src_ref, dest_ref,
    tree_ref, send_ref, root_ref, both, stack, coeff, picked, made,
):
    leaf_dev, rank, _ = bases_ref.shape
    to_tree(vec_ref, pts_ref, perm_ref, bases_ref, tree_ref, 0, both, stack, coeff)
    climb(leaf_dev, rank, trans_ref, coeff)
    top = (2 * leaf_dev - 2) * 8
    root_ref[...] = coeff[top : top + 8, :]
    couple(peers, blocks_ref, src_ref, dest_ref, coeff, picked, made, send_ref)


def upper(peers, rank, ups, up_t, up_c):
    offset, number = 0, peers
    device = lax.axis_index("leaf")

    def at(node):
        return pl.ds(pl.multiple_of(node * 8, 8), 8)

    gains = []
    while number > 1:
        node = device // (peers // number)
        sibling = node + 1 - 2 * (node % 2)
        partner = ups[at(offset + sibling), :rank]
        gains.append((offset + node, wide(nn, partner, up_c[offset + node])))
        if number > 2:

            def pair(parent, carry, offset=offset, number=number):
                total = 0.0
                for side in range(2):
                    child = offset + 2 * parent + side
                    total = total + wide(nn, ups[at(child), :rank], up_t[child])
                ups[at(offset + number + parent), :] = twice(total)
                return carry

            lax.fori_loop(0, number // 2, pair, 0, unroll=min(8, number // 2))
        offset += number
        number //= 2
    top = gains[-1][1]
    for node, gain in reversed(gains[:-1]):
        top = wide(nt, top, up_t[node]) + gain
    return top


def near_features(ext, fa, fb, leaf, leaf_len):
    cols = leaf_columns(leaf, leaf_len)
    place = ext[:, cols].astype(f32)[8:]
    square = place[0:1] * place[0:1] + place[1:2] * place[1:2]
    square = square + place[2:3] * place[2:3] + smooth_sq / 2
    high = square.astype(bf16).astype(f32)
    middle = (square - high).astype(bf16).astype(f32)
    low = square - high - middle
    row = lax.broadcasted_iota(i32, place.shape, 0)
    one = jnp.ones_like(place)
    first = jnp.where(row == 3, high, jnp.where(row == 4, middle, jnp.where(row == 5, low, one)))
    first = jnp.where(row < 3, -2.0 * place, first)
    second = jnp.where(row < 6, one, jnp.where(row == 6, high, middle))
    second = jnp.where(row < 3, place, second)
    last = row == 0
    fa[:, cols] = jnp.concatenate([first, jnp.where(last, one, 0.0)], axis=0).astype(bf16)
    fb[:, cols] = jnp.concatenate([second, jnp.where(last, low, 0.0)], axis=0).astype(bf16)


def near_pairs(ext, fa, fb, acc, leaf_len, source, targets, back):
    src = leaf_columns(source, leaf_len)
    for target in targets:
        tgt = leaf_columns(target, leaf_len)
        kernel = lax.rsqrt(tn(fa[:, src], fb[:, tgt])).astype(bf16)
        acc[:, tgt] += nn(ext[:, src], kernel)
        if back and target is not source:
            acc[:, src] += nt(ext[:, tgt], kernel)


def near_kernel(
    peers, leaf_len, left_ref, tree_ref, right_ref, roots_ref, up_t, up_c,
    near_ref, top_ref, ext, fa, fb, acc, ups,
):
    cols = tree_ref.shape[1]
    reach = NEAR * leaf_len
    leaf_dev = cols // leaf_len
    rank = up_t.shape[1]
    ups[: peers * 8, :] = roots_ref[...]
    top_ref[...] = upper(peers, rank, ups, up_t, up_c)
    ext[:, :reach] = left_ref[...]
    ext[:, reach : reach + cols] = tree_ref[...]
    ext[:, reach + cols :] = right_ref[...]
    acc[...] = jnp.zeros_like(acc)

    def features(leaf, carry):
        near_features(ext, fa, fb, leaf, leaf_len)
        return carry

    lax.fori_loop(0, leaf_dev + 2 * NEAR, features, 0)
    near_pairs(ext, fa, fb, acc, leaf_len, 0, (2,), False)
    near_pairs(ext, fa, fb, acc, leaf_len, 1, (2, 3), False)

    def body(leaf, carry):
        near_pairs(ext, fa, fb, acc, leaf_len, leaf, (leaf, leaf + 1, leaf + 2), True)
        return carry

    lax.fori_loop(NEAR, leaf_dev + NEAR, body, 0)
    near_ref[...] = acc[:8, reach : reach + cols] * (near_scale / leaf_len)


def finish_kernel(
    peers, recv_ref, top_ref, near_ref, trans_ref, bases_ref, perm_ref,
    out_ref, coupled, down, total,
):
    leaf_dev, rank, leaf_len = bases_ref.shape
    cols = perm_ref.shape[1]
    groups = cols // WIDTH

    def add(peer, value):
        rows = pl.ds(pl.multiple_of(peer * SLOTS, SLOTS), SLOTS)
        return value + recv_ref[rows, :].astype(f32)

    sums = lax.fori_loop(0, peers, add, jnp.zeros((SLOTS, 8 * rank), f32), unroll=4)
    for vec in range(8):
        coupled[pl.ds(vec, SLOTS, stride=8), :] = twice(sums[:, vec * rank : (vec + 1) * rank])
    top = (2 * leaf_dev - 2) * 8
    down[top : top + 8, :] = top_ref[...] + coupled[top : top + 8, :rank]
    number = 1
    while number < leaf_dev:
        above = 2 * leaf_dev - 2 * number
        number *= 2
        offset = 2 * leaf_dev - 2 * number
        for child in range(number):
            parent = (above + child // 2) * 8
            place = (offset + child) * 8
            down[place : place + 8, :] = (
                wide(nt, down[parent : parent + 8, :], trans_ref[offset + child])
                + coupled[place : place + 8, :rank]
            )
    total[...] = jnp.zeros_like(total)

    def one_leaf(leaf, carry):
        here = leaf_columns(leaf, leaf_len)
        perm = perm_ref[:, here]
        high = perm // WIDTH
        value = down[pl.ds(pl.multiple_of(leaf * 8, 8), 8), :].astype(bf16)
        tree = nn(value, bases_ref[leaf]) + near_ref[:, here]
        tree = tree.astype(bf16).astype(f32)
        masked = jnp.concatenate(
            [jnp.where(high == group, tree, 0.0) for group in range(groups)], axis=0
        ).astype(bf16)
        total[...] += nt(masked, one_hot(WIDTH, perm % WIDTH))
        return carry

    lax.fori_loop(0, leaf_dev, one_leaf, 0)
    for group in range(groups):
        out_ref[:, group * WIDTH : (group + 1) * WIDTH] = total[
            group * 8 : (group + 1) * 8, :
        ].astype(bf16)


params = pltpu.CompilerParams(vmem_limit_bytes=48 * 1024 * 1024)


def shape(dims, kind):
    return jax.ShapeDtypeStruct(dims, kind)


def shards(
    points, vectors, leaf_order, leaf_bases, transfers, coupling_blocks,
    block_source, block_owner, block_target, up_transfer, up_coupling,
):
    peers = lax.axis_size("leaf")
    leaf_dev, rank, leaf_len = leaf_bases.shape
    cols = vectors.shape[1]
    blocks = coupling_blocks.shape[0]
    reach = NEAR * leaf_len
    groups = cols // WIDTH
    source = block_source.reshape(1, blocks)
    dest = block_owner.reshape(1, blocks) * SLOTS + block_target.reshape(1, blocks)
    tree, send, root = pl.pallas_call(
        functools.partial(spread_kernel, peers),
        out_shape=(
            shape((ROWS, cols), bf16),
            shape((peers * SLOTS, 8 * rank), bf16),
            shape((8, 2 * rank), f32),
        ),
        scratch_shapes=[
            pltpu.VMEM((ROWS, cols), f32),
            pltpu.VMEM((groups * ROWS, WIDTH), bf16),
            pltpu.VMEM((SLOTS * 8, 2 * rank), f32),
            pltpu.VMEM((blocks * 8, 2 * rank), f32),
            pltpu.VMEM((blocks * 8, 2 * rank), f32),
        ],
        compiler_params=params,
        name="spread",
    )(vectors, points, leaf_order, leaf_bases, transfers, coupling_blocks, source, dest)
    received = lax.all_to_all(send, "leaf", split_axis=0, concat_axis=0, tiled=True)
    roots = lax.all_gather(root, "leaf", axis=0, tiled=True)
    up = [(i, i + 1) for i in range(peers - 1)]
    left = lax.ppermute(tree[:, cols - reach :], "leaf", up)
    right = lax.ppermute(tree[:, :reach], "leaf", [(j, i) for i, j in up])
    wide_cols = cols + 2 * reach
    near, top = pl.pallas_call(
        functools.partial(near_kernel, peers, leaf_len),
        out_shape=(shape((8, cols), f32), shape((8, rank), f32)),
        scratch_shapes=[
            pltpu.VMEM((ROWS, wide_cols), bf16),
            pltpu.VMEM((ROWS, wide_cols), bf16),
            pltpu.VMEM((ROWS, wide_cols), bf16),
            pltpu.VMEM((ROWS, wide_cols), f32),
            pltpu.VMEM((2 * peers * 8, 2 * rank), f32),
        ],
        compiler_params=params,
        cost_estimate=pl.CostEstimate(
            flops=30 * 10**9, bytes_accessed=10**6, transcendentals=14 * 10**6
        ),
        name="near",
    )(left, tree, right, roots, up_transfer, up_coupling)
    return pl.pallas_call(
        functools.partial(finish_kernel, peers),
        out_shape=shape((8, cols), bf16),
        scratch_shapes=[
            pltpu.VMEM((SLOTS * 8, 2 * rank), f32),
            pltpu.VMEM((SLOTS * 8, rank), f32),
            pltpu.VMEM((groups * 8, WIDTH), f32),
        ],
        compiler_params=params,
        name="finish",
    )(received, top, near, transfers, leaf_bases, leaf_order)


def solution(mesh):
    return jax.shard_map(
        shards,
        mesh=mesh,
        in_specs=(
            P(None, "leaf"),
            P("vec", "leaf"),
            P("leaf", None),
            P("leaf", None, None),
            P("leaf", None, None),
            P("leaf", None, None),
            P("leaf"),
            P("leaf", None),
            P("leaf"),
            P(),
            P(),
        ),
        out_specs=P("vec", "leaf"),
        check_vma=False,
    )
```

```python
import functools

import jax
import jax.numpy as jnp
from jax import lax
from jax.experimental import pallas as pl
from jax.experimental.pallas import tpu as pltpu
from jax.sharding import PartitionSpec as P

NEAR = 2
WIDTH = 256
SHIFT = 8
ROWS = 16
SLOTS = 32
near_scale = 8.0
smooth_sq = 0.0025
f32, bf16, i32 = jnp.float32, jnp.bfloat16, jnp.int32


def contract(left, right, dim_left, dim_right):
    return lax.dot_general(
        left, right, (((dim_left,), (dim_right,)), ((), ())), preferred_element_type=f32
    )


def nn(left, right):
    return contract(left, right, 1, 0)


def nt(left, right):
    return contract(left, right, 1, 1)


def tn(left, right):
    return contract(left, right, 0, 0)


def two_parts(value):
    high = value.astype(bf16).astype(f32)
    return jnp.concatenate([high, value - high], axis=0).astype(bf16)


def wide(product, value, matrix):
    count = value.shape[0]
    both = product(two_parts(value), matrix)
    return both[:count] + both[count:]


def one_hot(rows, index):
    ids = lax.broadcasted_iota(i32, (rows, index.shape[1]), 0)
    return jnp.where(ids == index, 1.0, 0.0).astype(bf16)


def twice(value):
    return jnp.concatenate([value, value], axis=1)


def leaf_columns(leaf, leaf_len):
    return pl.ds(pl.multiple_of(leaf * leaf_len, leaf_len), leaf_len)


def to_tree(vec_ref, pts_ref, perm_ref, bases_ref, tree_ref, tree_base, both, stack, coeff):
    local, cols = vec_ref.shape
    leaf_dev, rank, leaf_len = bases_ref.shape
    groups = cols // WIDTH
    both[...] = jnp.zeros_like(both)
    both[0:local] = vec_ref[...].astype(f32)
    both[8:11] = pts_ref[...].astype(f32)
    for group in range(groups):
        stack[group * ROWS : (group + 1) * ROWS, :] = both[
            :, group * WIDTH : (group + 1) * WIDTH
        ].astype(bf16)

    def one_leaf(leaf, carry):
        perm = perm_ref[:, leaf_columns(leaf, leaf_len)]
        high = lax.shift_right_logical(perm, SHIFT)
        picked = nn(stack[...], one_hot(WIDTH, perm & (WIDTH - 1)))
        total = jnp.where(high == 0, picked[:ROWS], 0.0)
        for group in range(1, groups):
            total = total + jnp.where(
                high == group, picked[group * ROWS : (group + 1) * ROWS], 0.0
            )
        tree = total.astype(bf16)
        tree_ref[:, leaf_columns(leaf + tree_base, leaf_len)] = tree
        own = nt(tree, bases_ref[leaf])[:local]
        coeff[pl.ds(pl.multiple_of(leaf * 8, 8), 8), :] = twice(own)
        return carry

    lax.fori_loop(0, leaf_dev, one_leaf, 0)


def climb(leaf_dev, rank, trans_ref, coeff):
    clusters = 2 * leaf_dev - 1
    coeff[clusters * 8 :, :] = jnp.zeros((coeff.shape[0] - clusters * 8, 2 * rank), f32)
    offset, number = 0, leaf_dev
    while number > 1:
        for parent in range(number // 2):
            total = 0.0
            for child in (offset + 2 * parent, offset + 2 * parent + 1):
                value = coeff[child * 8 : child * 8 + 8, :rank]
                total = total + wide(nn, value, trans_ref[child])
            place = (offset + number + parent) * 8
            coeff[place : place + 8, :] = twice(total)
        offset += number
        number //= 2


def couple(peers, blocks_ref, src_ref, dest, coeff, picked, made, send_ref):
    rank, _, blocks = blocks_ref.shape
    hot = one_hot(SLOTS, src_ref[...])
    for vec in range(8):
        values = coeff[pl.ds(vec, SLOTS, stride=8), :].astype(bf16)
        picked[vec * rank : (vec + 1) * rank, :] = tn(values, hot)[:rank]

    def part(block, carry):
        rows = pl.ds(pl.multiple_of(block * 16, 16), 16)

        def eight(step, sums):
            for inner in range(8):
                place = step * 8 + inner
                matrix = blocks_ref[place, rows, :].astype(f32)
                sums = tuple(
                    value + matrix * picked[pl.ds(vec * rank + place, 1), :]
                    for vec, value in enumerate(sums)
                )
            return sums

        zero = jnp.zeros((16, blocks), f32)
        sums = lax.fori_loop(0, rank // 8, eight, (zero,) * 8)
        for vec in range(8):
            place = pl.multiple_of(vec * rank + block * 16, 16)
            made[pl.ds(place, 16), :] = sums[vec].astype(bf16)
        return carry

    lax.fori_loop(0, rank // 16, part, 0)
    step_rows = 16 * SLOTS

    def some(step, carry):
        start = pl.multiple_of(step * step_rows, step_rows)
        send_ref[pl.ds(start, step_rows), :] = nt(
            one_hot(step_rows, dest - start), made[...]
        ).astype(bf16)
        return carry

    lax.fori_loop(0, peers * SLOTS // step_rows, some, 0)


def upper(peers, rank, ups, up_t, up_c):
    offset, number = 0, peers
    device = lax.axis_index("leaf")

    def at(node):
        return pl.ds(pl.multiple_of(node * 8, 8), 8)

    gains = []
    while number > 1:
        node = device // (peers // number)
        sibling = node + 1 - 2 * (node % 2)
        partner = ups[at(offset + sibling), :rank]
        gains.append((offset + node, wide(nn, partner, up_c[offset + node])))
        if number > 2:

            def pair(parent, carry, offset=offset, number=number):
                total = 0.0
                for side in range(2):
                    child = offset + 2 * parent + side
                    total = total + wide(nn, ups[at(child), :rank], up_t[child])
                ups[at(offset + number + parent), :] = twice(total)
                return carry

            lax.fori_loop(0, number // 2, pair, 0, unroll=min(8, number // 2))
        offset += number
        number //= 2
    top = gains[-1][1]
    for node, gain in reversed(gains[:-1]):
        top = wide(nt, top, up_t[node]) + gain
    return top


def near_features(mine, other, vx, fa, fb, cols):
    mine = mine.astype(f32)
    other = other.astype(f32)
    vx[:, cols] = jnp.concatenate([mine[:8], other[:8]], axis=0).astype(bf16)
    place = mine[8:]
    square = place[0:1] * place[0:1] + place[1:2] * place[1:2]
    square = square + place[2:3] * place[2:3] + smooth_sq / 2
    high = square.astype(bf16).astype(f32)
    middle = (square - high).astype(bf16).astype(f32)
    low = square - high - middle
    row = lax.broadcasted_iota(i32, place.shape, 0)
    one = jnp.ones_like(place)
    first = jnp.where(row == 3, high, jnp.where(row == 4, middle, jnp.where(row == 5, low, one)))
    first = jnp.where(row < 3, -2.0 * place, first)
    second = jnp.where(row < 6, one, jnp.where(row == 6, high, middle))
    second = jnp.where(row < 3, place, second)
    last = row == 0
    fa[:, cols] = jnp.concatenate([first, jnp.where(last, one, 0.0)], axis=0).astype(bf16)
    fb[:, cols] = jnp.concatenate([second, jnp.where(last, low, 0.0)], axis=0).astype(bf16)


def near_pairs(ext, fa, fb, acc, leaf_len, source, targets, back):
    src = leaf_columns(source, leaf_len)
    for target in targets:
        tgt = leaf_columns(target, leaf_len)
        kernel = lax.rsqrt(tn(fa[:, src], fb[:, tgt])).astype(bf16)
        acc[:, tgt] += nn(ext[:, src], kernel)
        if back and target is not source:
            acc[:, src] += nt(ext[:, tgt], kernel)


def finish(
    top_value, sums, near_all, trans_ref, bases_ref, perm_ref, out_ref, coupled, down, total
):
    leaf_dev, rank, leaf_len = bases_ref.shape
    cols = perm_ref.shape[1]
    groups = cols // WIDTH
    for vec in range(8):
        coupled[pl.ds(vec, SLOTS, stride=8), :] = twice(sums[:, vec * rank : (vec + 1) * rank])
    top = (2 * leaf_dev - 2) * 8
    down[top : top + 8, :] = top_value + coupled[top : top + 8, :rank]
    number = 1
    while number < leaf_dev:
        above = 2 * leaf_dev - 2 * number
        number *= 2
        offset = 2 * leaf_dev - 2 * number
        for child in range(number):
            parent = (above + child // 2) * 8
            place = (offset + child) * 8
            down[place : place + 8, :] = (
                wide(nt, down[parent : parent + 8, :], trans_ref[offset + child])
                + coupled[place : place + 8, :rank]
            )
    total[...] = jnp.zeros_like(total)

    def one_leaf(leaf, carry):
        here = leaf_columns(leaf, leaf_len)
        perm = perm_ref[:, here]
        high = lax.shift_right_logical(perm, SHIFT)
        value = down[pl.ds(pl.multiple_of(leaf * 8, 8), 8), :].astype(bf16)
        tree = nn(value, bases_ref[leaf]) + near_all[:, here] * (near_scale / leaf_len)
        tree = tree.astype(bf16).astype(f32)
        masked = jnp.concatenate(
            [jnp.where(high == group, tree, 0.0) for group in range(groups)], axis=0
        ).astype(bf16)
        total[...] += nt(masked, one_hot(WIDTH, perm & (WIDTH - 1)))
        return carry

    lax.fori_loop(0, leaf_dev, one_leaf, 0)
    for group in range(groups):
        out_ref[:, group * WIDTH : (group + 1) * WIDTH] = total[
            group * 8 : (group + 1) * 8, :
        ].astype(bf16)


def remote(source, target, send_sem, recv_sem, leaf, vec):
    return pltpu.make_async_remote_copy(
        src_ref=source,
        dst_ref=target,
        send_sem=send_sem,
        recv_sem=recv_sem,
        device_id=(leaf, vec),
        device_id_type=pl.DeviceIdType.MESH,
    )


def whole_kernel(
    peers, leaf_len, vec_ref, pts_ref, perm_ref, src_ref, owner_ref, target_ref,
    bases_any, trans_any, blocks_any, up_t_any, up_c_any, out_ref,
    bases, trans, blocks, up_t, up_c, both, stack, coeff, picked, made, send, recv, roots, ups,
    mine, other, halo, vx, fa, fb, acc, near_all, coupled, down, total,
    local_sem, part_sem, halo_send, halo_recv, root_send, root_recv, block_send, block_recv,
):
    cols = vec_ref.shape[1]
    leaf_dev = cols // leaf_len
    rank = trans_any.shape[1]
    reach = NEAR * leaf_len
    half = leaf_dev // 2
    device = lax.axis_index("leaf")
    core = lax.axis_index("vec")
    partner = 1 - core
    cross = device - 1 + 2 * core
    has_cross = jnp.logical_and(cross >= 0, cross < peers)
    barrier = pltpu.get_barrier_semaphore()

    def greet(leaf, vec):
        pl.semaphore_signal(
            barrier, inc=1, device_id=(leaf, vec), device_id_type=pl.DeviceIdType.MESH
        )

    def each_peer(work):
        def body(step, carry):
            work(lax.rem(device + step, peers))
            return carry

        lax.fori_loop(1, peers, body, 0)

    each_peer(lambda peer: greet(peer, core))
    greet(device, partner)

    @pl.when(has_cross)
    def _():
        greet(cross, partner)

    loads = [
        pltpu.make_async_copy(source, target, local_sem.at[place])
        for place, (source, target) in enumerate(
            [(bases_any, bases), (trans_any, trans), (blocks_any, blocks), (up_t_any, up_t),
             (up_c_any, up_c)]
        )
    ]
    for load in loads:
        load.start()
    loads[0].wait()
    to_tree(vec_ref, pts_ref, perm_ref, bases, mine, 0, both, stack, coeff)
    pl.semaphore_wait(barrier, peers + jnp.where(has_cross, 1, 0))

    seen = (half + NEAR) * leaf_len
    shift = (half - NEAR) * leaf_len
    to_partner = remote(
        mine.at[:, pl.ds(pl.multiple_of(partner * shift, 128), seen)], other,
        part_sem.at[0], part_sem.at[1], device, partner,
    )
    to_partner.start()
    to_right = remote(
        mine.at[:, cols - reach :], halo.at[core], halo_send.at[0], halo_recv.at[core],
        device + 1, 0,
    )
    to_left = remote(
        mine.at[:, :reach], halo.at[core], halo_send.at[1], halo_recv.at[core], device - 1, 1
    )
    not_last = device < peers - 1
    not_first = device > 0

    @pl.when(not_last)
    def _():
        to_right.start()

    @pl.when(not_first)
    def _():
        to_left.start()

    loads[1].wait()
    climb(leaf_dev, rank, trans, coeff)
    top = (2 * leaf_dev - 2) * 8
    mine_rows = pl.ds(pl.multiple_of(device * 8, 8), 8)
    ups[mine_rows, :] = coeff[top : top + 8, :]

    def root_copy(peer, place):
        return remote(
            coeff.at[top : top + 8, :], roots.at[place], root_send.at[peer],
            root_recv.at[place], peer, core,
        )

    each_peer(lambda peer: root_copy(peer, device).start())
    loads[2].wait()
    dest = owner_ref[...] * SLOTS + target_ref[...]
    couple(peers, blocks, src_ref, dest, coeff, picked, made, send)

    def slot(place):
        return pl.ds(pl.multiple_of(place * SLOTS, SLOTS), SLOTS)

    def block_copy(peer, place):
        return remote(
            send.at[slot(peer), :], recv.at[slot(place), :], block_send.at[peer],
            block_recv.at[place], peer, core,
        )

    each_peer(lambda peer: block_copy(peer, device).start())

    to_partner.wait_recv()
    off = NEAR * (1 - core)

    def features(place, carry):
        here = leaf_columns(place, leaf_len)
        there = leaf_columns(place + core * (half - NEAR), leaf_len)
        near_features(
            mine[:, there], other[:, here], vx, fa, fb, leaf_columns(place + off, leaf_len)
        )
        return carry

    lax.fori_loop(0, half + NEAR, features, 0)

    @pl.when(has_cross)
    def _():
        for vec in range(2):
            remote(
                mine.at[:, :reach], halo.at[vec], halo_send.at[vec], halo_recv.at[vec],
                device, partner,
            ).wait_recv()

    @pl.when(jnp.logical_not(has_cross))
    def _():
        halo[...] = jnp.zeros_like(halo)

    for place in range(NEAR):
        here = slice(place * leaf_len, (place + 1) * leaf_len)
        near_features(
            halo[core, :, here], halo[partner, :, here], vx, fa, fb,
            leaf_columns(place + core * (half + NEAR), leaf_len),
        )
    acc[...] = jnp.zeros_like(acc)
    near_pairs(vx, fa, fb, acc, leaf_len, 0, (2,), False)
    near_pairs(vx, fa, fb, acc, leaf_len, 1, (2, 3), False)

    def body(leaf, carry):
        near_pairs(vx, fa, fb, acc, leaf_len, leaf, (leaf, leaf + 1, leaf + 2), True)
        return carry

    lax.fori_loop(NEAR, half + NEAR, body, 0)
    part = half * leaf_len
    computed = pl.ds(pl.multiple_of(core * part, 128), part)
    to_near = remote(
        acc.at[8:16, pl.ds(reach, part)], near_all.at[:, computed],
        part_sem.at[2], part_sem.at[3], device, partner,
    )
    to_near.start()
    near_all[:, computed] = acc[:8, reach : reach + part]

    loads[3].wait()
    loads[4].wait()

    def root_in(peer):
        root_copy(peer, peer).wait_recv()
        ups[pl.ds(pl.multiple_of(peer * 8, 8), 8), :] = roots[peer]

    each_peer(root_in)
    top_value = upper(peers, rank, ups, up_t, up_c)

    def add(step, value):
        peer = lax.rem(device + step, peers)
        block_copy(peer, peer).wait_recv()
        return value + recv[slot(peer), :].astype(f32)

    sums = lax.fori_loop(1, peers, add, send[slot(device), :].astype(f32))
    to_near.wait_recv()
    finish(top_value, sums, near_all, trans, bases, perm_ref, out_ref, coupled, down, total)

    to_partner.wait_send()
    to_near.wait_send()

    @pl.when(not_last)
    def _():
        to_right.wait_send()

    @pl.when(not_first)
    def _():
        to_left.wait_send()

    def sent(peer):
        root_copy(peer, device).wait_send()
        block_copy(peer, device).wait_send()

    each_peer(sent)


def shards(
    points, vectors, leaf_order, leaf_bases, transfers, coupling_blocks,
    block_source, block_owner, block_target, up_transfer, up_coupling,
):
    peers = lax.axis_size("leaf")
    leaf_dev, rank, leaf_len = leaf_bases.shape
    cols = vectors.shape[1]
    blocks = coupling_blocks.shape[0]
    reach = NEAR * leaf_len
    groups = cols // WIDTH
    half = leaf_dev // 2
    span = (half + 2 * NEAR) * leaf_len
    by_block = jnp.transpose(coupling_blocks, (1, 2, 0))
    vmem = pl.BlockSpec(memory_space=pltpu.VMEM)
    anywhere = pl.BlockSpec(memory_space=pl.ANY)
    dma = pltpu.SemaphoreType.DMA
    return pl.pallas_call(
        functools.partial(whole_kernel, peers, leaf_len),
        out_shape=jax.ShapeDtypeStruct((8, cols), bf16),
        in_specs=[vmem] * 6 + [anywhere] * 5,
        out_specs=vmem,
        scratch_shapes=[
            pltpu.VMEM(leaf_bases.shape, bf16),
            pltpu.VMEM(transfers.shape, bf16),
            pltpu.VMEM(by_block.shape, bf16),
            pltpu.VMEM(up_transfer.shape, bf16),
            pltpu.VMEM(up_coupling.shape, bf16),
            pltpu.VMEM((ROWS, cols), f32),
            pltpu.VMEM((groups * ROWS, WIDTH), bf16),
            pltpu.VMEM((SLOTS * 8, 2 * rank), f32),
            pltpu.VMEM((8 * rank, blocks), f32),
            pltpu.VMEM((8 * rank, blocks), bf16),
            pltpu.VMEM((peers * SLOTS, 8 * rank), bf16),
            pltpu.VMEM((peers * SLOTS, 8 * rank), bf16),
            pltpu.VMEM((peers, 8, 2 * rank), f32),
            pltpu.VMEM((2 * peers * 8, 2 * rank), f32),
            pltpu.VMEM((ROWS, cols), bf16),
            pltpu.VMEM((ROWS, (half + NEAR) * leaf_len), bf16),
            pltpu.VMEM((2, ROWS, reach), bf16),
            pltpu.VMEM((ROWS, span), bf16),
            pltpu.VMEM((ROWS, span), bf16),
            pltpu.VMEM((ROWS, span), bf16),
            pltpu.VMEM((ROWS, span), f32),
            pltpu.VMEM((8, cols), f32),
            pltpu.VMEM((SLOTS * 8, 2 * rank), f32),
            pltpu.VMEM((SLOTS * 8, rank), f32),
            pltpu.VMEM((groups * 8, WIDTH), f32),
            dma((5,)),
            dma((4,)),
            dma((2,)),
            dma((2,)),
            dma((peers,)),
            dma((peers,)),
            dma((peers,)),
            dma((peers,)),
        ],
        compiler_params=pltpu.CompilerParams(
            vmem_limit_bytes=48 * 1024 * 1024, collective_id=0, has_side_effects=True
        ),
        name="whole",
    )(
        vectors, points, leaf_order,
        block_source.reshape(1, blocks), block_owner.reshape(1, blocks),
        block_target.reshape(1, blocks),
        leaf_bases, transfers, by_block, up_transfer, up_coupling,
    )


def solution(mesh):
    return jax.shard_map(
        shards,
        mesh=mesh,
        in_specs=(
            P(None, "leaf"),
            P("vec", "leaf"),
            P("leaf", None),
            P("leaf", None, None),
            P("leaf", None, None),
            P("leaf", None, None),
            P("leaf"),
            P("leaf", None),
            P("leaf"),
            P(),
            P(),
        ),
        out_specs=P("vec", "leaf"),
        check_vma=False,
    )
```

```python
import functools

import jax
import jax.numpy as jnp
from jax import lax
from jax.experimental import pallas as pl
from jax.experimental.pallas import tpu as pltpu
from jax.sharding import PartitionSpec as P

NEAR = 2
WIDTH = 256
SHIFT = 8
ROWS = 16
SLOTS = 32
near_scale = 8.0
smooth_sq = 0.0025
f32, bf16, i32 = jnp.float32, jnp.bfloat16, jnp.int32


def contract(left, right, dim_left, dim_right):
    return lax.dot_general(
        left, right, (((dim_left,), (dim_right,)), ((), ())), preferred_element_type=f32
    )


def nn(left, right):
    return contract(left, right, 1, 0)


def nt(left, right):
    return contract(left, right, 1, 1)


def tn(left, right):
    return contract(left, right, 0, 0)


def two_parts(value):
    high = value.astype(bf16).astype(f32)
    return jnp.concatenate([high, value - high], axis=0).astype(bf16)


def wide(product, value, matrix):
    count = value.shape[0]
    both = product(two_parts(value), matrix)
    return both[:count] + both[count:]


def one_hot(rows, index):
    ids = lax.broadcasted_iota(i32, (rows, index.shape[1]), 0)
    return jnp.where(ids == index, 1.0, 0.0).astype(bf16)


def twice(value):
    return jnp.concatenate([value, value], axis=1)


def leaf_columns(leaf, leaf_len):
    return pl.ds(pl.multiple_of(leaf * leaf_len, leaf_len), leaf_len)


def to_tree(vec_ref, pts_ref, perm_ref, bases_ref, tree_ref, tree_base, both, stack, coeff):
    local, cols = vec_ref.shape
    leaf_dev, rank, leaf_len = bases_ref.shape
    groups = cols // WIDTH
    both[...] = jnp.zeros_like(both)
    both[0:local] = vec_ref[...].astype(f32)
    both[8:11] = pts_ref[...].astype(f32)
    for group in range(groups):
        stack[group * ROWS : (group + 1) * ROWS, :] = both[
            :, group * WIDTH : (group + 1) * WIDTH
        ].astype(bf16)

    def one_leaf(leaf, carry):
        perm = perm_ref[:, leaf_columns(leaf, leaf_len)]
        high = lax.shift_right_logical(perm, SHIFT)
        picked = nn(stack[...], one_hot(WIDTH, perm & (WIDTH - 1)))
        total = jnp.where(high == 0, picked[:ROWS], 0.0)
        for group in range(1, groups):
            total = total + jnp.where(
                high == group, picked[group * ROWS : (group + 1) * ROWS], 0.0
            )
        tree = total.astype(bf16)
        tree_ref[:, leaf_columns(leaf + tree_base, leaf_len)] = tree
        own = nt(tree, bases_ref[leaf])[:local]
        coeff[pl.ds(pl.multiple_of(leaf * 8, 8), 8), :] = twice(own)
        return carry

    lax.fori_loop(0, leaf_dev, one_leaf, 0, unroll=4)


def climb(leaf_dev, rank, trans_ref, coeff):
    clusters = 2 * leaf_dev - 1
    coeff[clusters * 8 :, :] = jnp.zeros((coeff.shape[0] - clusters * 8, 2 * rank), f32)
    offset, number = 0, leaf_dev
    while number > 1:
        for parent in range(number // 2):
            total = 0.0
            for child in (offset + 2 * parent, offset + 2 * parent + 1):
                value = coeff[child * 8 : child * 8 + 8, :rank]
                total = total + wide(nn, value, trans_ref[child])
            place = (offset + number + parent) * 8
            coeff[place : place + 8, :] = twice(total)
        offset += number
        number //= 2


def couple(peers, blocks_ref, src_ref, dest, coeff, picked, made, send_ref):
    rank, _, blocks = blocks_ref.shape
    hot = one_hot(SLOTS, src_ref[...])
    for vec in range(8):
        values = coeff[pl.ds(vec, SLOTS, stride=8), :].astype(bf16)
        picked[vec * rank : (vec + 1) * rank, :] = tn(values, hot)[:rank]

    def part(block, carry):
        rows = pl.ds(pl.multiple_of(block * 16, 16), 16)

        def eight(step, sums):
            for inner in range(8):
                place = step * 8 + inner
                matrix = blocks_ref[place, rows, :].astype(f32)
                sums = tuple(
                    value + matrix * picked[pl.ds(vec * rank + place, 1), :]
                    for vec, value in enumerate(sums)
                )
            return sums

        zero = jnp.zeros((16, blocks), f32)
        sums = lax.fori_loop(0, rank // 8, eight, (zero,) * 8)
        for vec in range(8):
            place = pl.multiple_of(vec * rank + block * 16, 16)
            made[pl.ds(place, 16), :] = sums[vec].astype(bf16)
        return carry

    lax.fori_loop(0, rank // 16, part, 0)
    step_rows = 16 * SLOTS

    def some(step, carry):
        start = pl.multiple_of(step * step_rows, step_rows)
        send_ref[pl.ds(start, step_rows), :] = nt(
            one_hot(step_rows, dest - start), made[...]
        ).astype(bf16)
        return carry

    lax.fori_loop(0, peers * SLOTS // step_rows, some, 0)


def upper(peers, rank, ups, up_t, up_c):
    offset, number = 0, peers
    device = lax.axis_index("leaf")

    def at(node):
        return pl.ds(pl.multiple_of(node * 8, 8), 8)

    gains = []
    while number > 1:
        node = device // (peers // number)
        sibling = node + 1 - 2 * (node % 2)
        partner = ups[at(offset + sibling), :rank]
        gains.append((offset + node, wide(nn, partner, up_c[offset + node])))
        if number > 2:

            def pair(parent, carry, offset=offset, number=number):
                total = 0.0
                for side in range(2):
                    child = offset + 2 * parent + side
                    total = total + wide(nn, ups[at(child), :rank], up_t[child])
                ups[at(offset + number + parent), :] = twice(total)
                return carry

            lax.fori_loop(0, number // 2, pair, 0, unroll=min(8, number // 2))
        offset += number
        number //= 2
    top = gains[-1][1]
    for node, gain in reversed(gains[:-1]):
        top = wide(nt, top, up_t[node]) + gain
    return top


def near_features(mine, other, vx, fa, fb, cols):
    mine = mine.astype(f32)
    other = other.astype(f32)
    vx[:, cols] = jnp.concatenate([mine[:8], other[:8]], axis=0).astype(bf16)
    place = mine[8:]
    square = place[0:1] * place[0:1] + place[1:2] * place[1:2]
    square = square + place[2:3] * place[2:3] + smooth_sq / 2
    high = square.astype(bf16).astype(f32)
    middle = (square - high).astype(bf16).astype(f32)
    low = square - high - middle
    row = lax.broadcasted_iota(i32, place.shape, 0)
    one = jnp.ones_like(place)
    first = jnp.where(row == 3, high, jnp.where(row == 4, middle, jnp.where(row == 5, low, one)))
    first = jnp.where(row < 3, -2.0 * place, first)
    second = jnp.where(row < 6, one, jnp.where(row == 6, high, middle))
    second = jnp.where(row < 3, place, second)
    last = row == 0
    fa[:, cols] = jnp.concatenate([first, jnp.where(last, one, 0.0)], axis=0).astype(bf16)
    fb[:, cols] = jnp.concatenate([second, jnp.where(last, low, 0.0)], axis=0).astype(bf16)


def near_pairs(ext, fa, fb, acc, leaf_len, source, targets, back):
    src = leaf_columns(source, leaf_len)
    for target in targets:
        tgt = leaf_columns(target, leaf_len)
        kernel = lax.rsqrt(tn(fa[:, src], fb[:, tgt])).astype(bf16)
        acc[:, tgt] += nn(ext[:, src], kernel)
        if back and target is not source:
            acc[:, src] += nt(ext[:, tgt], kernel)


def finish(
    top_value, sums, near_all, trans_ref, bases_ref, perm_ref, out_ref, coupled, down, total
):
    leaf_dev, rank, leaf_len = bases_ref.shape
    cols = perm_ref.shape[1]
    groups = cols // WIDTH
    for vec in range(8):
        coupled[pl.ds(vec, SLOTS, stride=8), :] = twice(sums[:, vec * rank : (vec + 1) * rank])
    top = (2 * leaf_dev - 2) * 8
    down[top : top + 8, :] = top_value + coupled[top : top + 8, :rank]
    number = 1
    while number < leaf_dev:
        above = 2 * leaf_dev - 2 * number
        number *= 2
        offset = 2 * leaf_dev - 2 * number
        for child in range(number):
            parent = (above + child // 2) * 8
            place = (offset + child) * 8
            down[place : place + 8, :] = (
                wide(nt, down[parent : parent + 8, :], trans_ref[offset + child])
                + coupled[place : place + 8, :rank]
            )
    total[...] = jnp.zeros_like(total)

    def one_leaf(leaf, carry):
        here = leaf_columns(leaf, leaf_len)
        perm = perm_ref[:, here]
        high = lax.shift_right_logical(perm, SHIFT)
        value = down[pl.ds(pl.multiple_of(leaf * 8, 8), 8), :].astype(bf16)
        tree = nn(value, bases_ref[leaf]) + near_all[:, here] * (near_scale / leaf_len)
        tree = tree.astype(bf16).astype(f32)
        masked = jnp.concatenate(
            [jnp.where(high == group, tree, 0.0) for group in range(groups)], axis=0
        ).astype(bf16)
        total[...] += nt(masked, one_hot(WIDTH, perm & (WIDTH - 1)))
        return carry

    lax.fori_loop(0, leaf_dev, one_leaf, 0, unroll=4)
    for group in range(groups):
        out_ref[:, group * WIDTH : (group + 1) * WIDTH] = total[
            group * 8 : (group + 1) * 8, :
        ].astype(bf16)


def remote(source, target, send_sem, recv_sem, leaf, vec):
    return pltpu.make_async_remote_copy(
        src_ref=source,
        dst_ref=target,
        send_sem=send_sem,
        recv_sem=recv_sem,
        device_id=(leaf, vec),
        device_id_type=pl.DeviceIdType.MESH,
    )


def whole_kernel(
    peers, leaf_len, vec_any, pts_any, perm_any, src_any, owner_any, target_any,
    bases_any, trans_any, blocks_any, up_t_any, up_c_any, out_ref,
    vec_ref, pts_ref, perm_ref, src_ref, owner_ref, target_ref, bases, trans, blocks, up_t, up_c, both, stack, coeff, picked, made, send, recv, roots, ups,
    mine, other, halo, vx, fa, fb, acc, near_all, coupled, down, total,
    local_sem, part_sem, halo_send, halo_recv, root_send, root_recv, block_send, block_recv,
):
    cols = vec_any.shape[1]
    leaf_dev = cols // leaf_len
    rank = trans_any.shape[1]
    reach = NEAR * leaf_len
    half = leaf_dev // 2
    device = lax.axis_index("leaf")
    core = lax.axis_index("vec")
    partner = 1 - core
    cross = device - 1 + 2 * core
    has_cross = jnp.logical_and(cross >= 0, cross < peers)
    barrier = pltpu.get_barrier_semaphore()

    def greet(leaf, vec):
        pl.semaphore_signal(
            barrier, inc=1, device_id=(leaf, vec), device_id_type=pl.DeviceIdType.MESH
        )

    def each_peer(work):
        def body(step, carry):
            work(lax.rem(device + step, peers))
            return carry

        lax.fori_loop(1, peers, body, 0)

    each_peer(lambda peer: greet(peer, core))
    greet(device, partner)

    @pl.when(has_cross)
    def _():
        greet(cross, partner)

    loads = [
        pltpu.make_async_copy(source, target, local_sem.at[place])
        for place, (source, target) in enumerate(
            [(perm_any, perm_ref), (vec_any, vec_ref), (pts_any, pts_ref), (bases_any, bases),
             (trans_any, trans), (src_any, src_ref), (blocks_any, blocks),
             (owner_any, owner_ref), (target_any, target_ref), (up_t_any, up_t),
             (up_c_any, up_c)]
        )
    ]
    for load in loads:
        load.start()
    for load in loads[:4]:
        load.wait()
    to_tree(vec_ref, pts_ref, perm_ref, bases, mine, 0, both, stack, coeff)
    pl.semaphore_wait(barrier, peers + jnp.where(has_cross, 1, 0))

    seen = (half + NEAR) * leaf_len
    shift = (half - NEAR) * leaf_len
    to_partner = remote(
        mine.at[:, pl.ds(pl.multiple_of(partner * shift, 128), seen)], other,
        part_sem.at[0], part_sem.at[1], device, partner,
    )
    to_partner.start()
    to_right = remote(
        mine.at[:, cols - reach :], halo.at[core], halo_send.at[0], halo_recv.at[core],
        device + 1, 0,
    )
    to_left = remote(
        mine.at[:, :reach], halo.at[core], halo_send.at[1], halo_recv.at[core], device - 1, 1
    )
    not_last = device < peers - 1
    not_first = device > 0

    @pl.when(not_last)
    def _():
        to_right.start()

    @pl.when(not_first)
    def _():
        to_left.start()

    loads[4].wait()
    climb(leaf_dev, rank, trans, coeff)
    top = (2 * leaf_dev - 2) * 8
    mine_rows = pl.ds(pl.multiple_of(device * 8, 8), 8)
    ups[mine_rows, :] = coeff[top : top + 8, :]

    def root_copy(peer, place):
        return remote(
            coeff.at[top : top + 8, :], roots.at[place], root_send.at[peer],
            root_recv.at[place], peer, core,
        )

    each_peer(lambda peer: root_copy(peer, device).start())
    for load in loads[5:9]:
        load.wait()
    dest = owner_ref[...] * SLOTS + target_ref[...]
    couple(peers, blocks, src_ref, dest, coeff, picked, made, send)

    def slot(place):
        return pl.ds(pl.multiple_of(place * SLOTS, SLOTS), SLOTS)

    def block_copy(peer, place):
        return remote(
            send.at[slot(peer), :], recv.at[slot(place), :], block_send.at[peer],
            block_recv.at[place], peer, core,
        )

    each_peer(lambda peer: block_copy(peer, device).start())

    to_partner.wait_recv()
    off = NEAR * (1 - core)

    def features(place, carry):
        here = leaf_columns(place, leaf_len)
        there = leaf_columns(place + core * (half - NEAR), leaf_len)
        near_features(
            mine[:, there], other[:, here], vx, fa, fb, leaf_columns(place + off, leaf_len)
        )
        return carry

    lax.fori_loop(0, half + NEAR, features, 0)

    @pl.when(has_cross)
    def _():
        for vec in range(2):
            remote(
                mine.at[:, :reach], halo.at[vec], halo_send.at[vec], halo_recv.at[vec],
                device, partner,
            ).wait_recv()

    @pl.when(jnp.logical_not(has_cross))
    def _():
        halo[...] = jnp.zeros_like(halo)

    for place in range(NEAR):
        here = slice(place * leaf_len, (place + 1) * leaf_len)
        near_features(
            halo[core, :, here], halo[partner, :, here], vx, fa, fb,
            leaf_columns(place + core * (half + NEAR), leaf_len),
        )
    acc[...] = jnp.zeros_like(acc)
    near_pairs(vx, fa, fb, acc, leaf_len, 0, (2,), False)
    near_pairs(vx, fa, fb, acc, leaf_len, 1, (2, 3), False)

    def body(leaf, carry):
        near_pairs(vx, fa, fb, acc, leaf_len, leaf, (leaf, leaf + 1, leaf + 2), True)
        return carry

    lax.fori_loop(NEAR, half + NEAR, body, 0)
    part = half * leaf_len
    computed = pl.ds(pl.multiple_of(core * part, 128), part)
    to_near = remote(
        acc.at[8:16, pl.ds(reach, part)], near_all.at[:, computed],
        part_sem.at[2], part_sem.at[3], device, partner,
    )
    to_near.start()
    near_all[:, computed] = acc[:8, reach : reach + part]

    loads[9].wait()
    loads[10].wait()

    def root_in(peer):
        root_copy(peer, peer).wait_recv()
        ups[pl.ds(pl.multiple_of(peer * 8, 8), 8), :] = roots[peer]

    each_peer(root_in)
    top_value = upper(peers, rank, ups, up_t, up_c)

    def add(step, value):
        peer = lax.rem(device + step, peers)
        block_copy(peer, peer).wait_recv()
        return value + recv[slot(peer), :].astype(f32)

    sums = lax.fori_loop(1, peers, add, send[slot(device), :].astype(f32))
    to_near.wait_recv()
    finish(top_value, sums, near_all, trans, bases, perm_ref, out_ref, coupled, down, total)

    to_partner.wait_send()
    to_near.wait_send()

    @pl.when(not_last)
    def _():
        to_right.wait_send()

    @pl.when(not_first)
    def _():
        to_left.wait_send()

    def sent(peer):
        root_copy(peer, device).wait_send()
        block_copy(peer, device).wait_send()

    each_peer(sent)


def shards(
    points, vectors, leaf_order, leaf_bases, transfers, coupling_blocks,
    block_source, block_owner, block_target, up_transfer, up_coupling,
):
    peers = lax.axis_size("leaf")
    leaf_dev, rank, leaf_len = leaf_bases.shape
    cols = vectors.shape[1]
    blocks = coupling_blocks.shape[0]
    reach = NEAR * leaf_len
    groups = cols // WIDTH
    half = leaf_dev // 2
    span = (half + 2 * NEAR) * leaf_len
    by_block = jnp.transpose(coupling_blocks, (1, 2, 0))
    vmem = pl.BlockSpec(memory_space=pltpu.VMEM)
    anywhere = pl.BlockSpec(memory_space=pl.ANY)
    dma = pltpu.SemaphoreType.DMA
    return pl.pallas_call(
        functools.partial(whole_kernel, peers, leaf_len),
        out_shape=jax.ShapeDtypeStruct((8, cols), bf16),
        in_specs=[anywhere] * 11,
        out_specs=vmem,
        scratch_shapes=[
            pltpu.VMEM(vectors.shape, bf16),
            pltpu.VMEM(points.shape, bf16),
            pltpu.VMEM(leaf_order.shape, i32),
            pltpu.VMEM((1, blocks), i32),
            pltpu.VMEM((1, blocks), i32),
            pltpu.VMEM((1, blocks), i32),
            pltpu.VMEM(leaf_bases.shape, bf16),
            pltpu.VMEM(transfers.shape, bf16),
            pltpu.VMEM(by_block.shape, bf16),
            pltpu.VMEM(up_transfer.shape, bf16),
            pltpu.VMEM(up_coupling.shape, bf16),
            pltpu.VMEM((ROWS, cols), f32),
            pltpu.VMEM((groups * ROWS, WIDTH), bf16),
            pltpu.VMEM((SLOTS * 8, 2 * rank), f32),
            pltpu.VMEM((8 * rank, blocks), f32),
            pltpu.VMEM((8 * rank, blocks), bf16),
            pltpu.VMEM((peers * SLOTS, 8 * rank), bf16),
            pltpu.VMEM((peers * SLOTS, 8 * rank), bf16),
            pltpu.VMEM((peers, 8, 2 * rank), f32),
            pltpu.VMEM((2 * peers * 8, 2 * rank), f32),
            pltpu.VMEM((ROWS, cols), bf16),
            pltpu.VMEM((ROWS, (half + NEAR) * leaf_len), bf16),
            pltpu.VMEM((2, ROWS, reach), bf16),
            pltpu.VMEM((ROWS, span), bf16),
            pltpu.VMEM((ROWS, span), bf16),
            pltpu.VMEM((ROWS, span), bf16),
            pltpu.VMEM((ROWS, span), f32),
            pltpu.VMEM((8, cols), f32),
            pltpu.VMEM((SLOTS * 8, 2 * rank), f32),
            pltpu.VMEM((SLOTS * 8, rank), f32),
            pltpu.VMEM((groups * 8, WIDTH), f32),
            dma((11,)),
            dma((4,)),
            dma((2,)),
            dma((2,)),
            dma((peers,)),
            dma((peers,)),
            dma((peers,)),
            dma((peers,)),
        ],
        compiler_params=pltpu.CompilerParams(
            vmem_limit_bytes=64 * 1024 * 1024, collective_id=0, has_side_effects=True
        ),
        name="whole",
    )(
        vectors, points, leaf_order,
        block_source.reshape(1, blocks), block_owner.reshape(1, blocks),
        block_target.reshape(1, blocks),
        leaf_bases, transfers, by_block, up_transfer, up_coupling,
    )


def solution(mesh):
    return jax.shard_map(
        shards,
        mesh=mesh,
        in_specs=(
            P(None, "leaf"),
            P("vec", "leaf"),
            P("leaf", None),
            P("leaf", None, None),
            P("leaf", None, None),
            P("leaf", None, None),
            P("leaf"),
            P("leaf", None),
            P("leaf"),
            P(),
            P(),
        ),
        out_specs=P("vec", "leaf"),
        check_vma=False,
    )
```

```python
import functools

import jax
import jax.numpy as jnp
from jax import lax
from jax.experimental import pallas as pl
from jax.experimental.pallas import tpu as pltpu
from jax.sharding import PartitionSpec as P

NEAR = 2
WIDTH = 256
SHIFT = 8
ROWS = 16
SLOTS = 32
near_scale = 8.0
smooth_sq = 0.0025
f32, bf16, i32 = jnp.float32, jnp.bfloat16, jnp.int32


def contract(left, right, dim_left, dim_right):
    return lax.dot_general(
        left, right, (((dim_left,), (dim_right,)), ((), ())), preferred_element_type=f32
    )


def nn(left, right):
    return contract(left, right, 1, 0)


def nt(left, right):
    return contract(left, right, 1, 1)


def tn(left, right):
    return contract(left, right, 0, 0)


def two_parts(value):
    high = value.astype(bf16).astype(f32)
    return jnp.concatenate([high, value - high], axis=0).astype(bf16)


def wide(product, value, matrix):
    count = value.shape[0]
    both = product(two_parts(value), matrix)
    return both[:count] + both[count:]


def one_hot(rows, index):
    ids = lax.broadcasted_iota(i32, (rows, index.shape[1]), 0)
    return jnp.where(ids == index, 1.0, 0.0).astype(bf16)


def twice(value):
    return jnp.concatenate([value, value], axis=1)


def leaf_columns(leaf, leaf_len):
    return pl.ds(pl.multiple_of(leaf * leaf_len, leaf_len), leaf_len)


def to_tree(vec_ref, pts_ref, perm_ref, bases_ref, tree_ref, tree_base, both, stack, coeff):
    local, cols = vec_ref.shape
    leaf_dev, rank, leaf_len = bases_ref.shape
    groups = cols // WIDTH
    both[...] = jnp.zeros_like(both)
    both[0:local] = vec_ref[...].astype(f32)
    both[8:11] = pts_ref[...].astype(f32)
    for group in range(groups):
        stack[group * ROWS : (group + 1) * ROWS, :] = both[
            :, group * WIDTH : (group + 1) * WIDTH
        ].astype(bf16)

    def one_leaf(leaf, carry):
        perm = perm_ref[:, leaf_columns(leaf, leaf_len)]
        high = lax.shift_right_logical(perm, SHIFT)
        picked = nn(stack[...], one_hot(WIDTH, perm & (WIDTH - 1)))
        total = jnp.where(high == 0, picked[:ROWS], 0.0)
        for group in range(1, groups):
            total = total + jnp.where(
                high == group, picked[group * ROWS : (group + 1) * ROWS], 0.0
            )
        tree = total.astype(bf16)
        tree_ref[:, leaf_columns(leaf + tree_base, leaf_len)] = tree
        own = nt(tree, bases_ref[leaf])[:local]
        coeff[pl.ds(pl.multiple_of(leaf * 8, 8), 8), :] = twice(own)
        return carry

    lax.fori_loop(0, leaf_dev, one_leaf, 0, unroll=4)


def climb(leaf_dev, rank, trans_ref, coeff):
    clusters = 2 * leaf_dev - 1
    coeff[clusters * 8 :, :] = jnp.zeros((coeff.shape[0] - clusters * 8, 2 * rank), f32)
    offset, number = 0, leaf_dev
    while number > 1:
        for parent in range(number // 2):
            total = 0.0
            for child in (offset + 2 * parent, offset + 2 * parent + 1):
                value = coeff[child * 8 : child * 8 + 8, :rank]
                total = total + wide(nn, value, trans_ref[child])
            place = (offset + number + parent) * 8
            coeff[place : place + 8, :] = twice(total)
        offset += number
        number //= 2


def couple(peers, blocks_ref, src_ref, dest, coeff, picked, made, send_ref):
    rank, _, blocks = blocks_ref.shape
    hot = one_hot(SLOTS, src_ref[...])
    for vec in range(8):
        values = coeff[pl.ds(vec, SLOTS, stride=8), :].astype(bf16)
        picked[vec * rank : (vec + 1) * rank, :] = tn(values, hot)[:rank]

    def part(block, carry):
        rows = pl.ds(pl.multiple_of(block * 16, 16), 16)

        def eight(step, sums):
            for inner in range(8):
                place = step * 8 + inner
                matrix = blocks_ref[place, rows, :].astype(f32)
                sums = tuple(
                    value + matrix * picked[pl.ds(vec * rank + place, 1), :]
                    for vec, value in enumerate(sums)
                )
            return sums

        zero = jnp.zeros((16, blocks), f32)
        sums = lax.fori_loop(0, rank // 8, eight, (zero,) * 8)
        for vec in range(8):
            place = pl.multiple_of(vec * rank + block * 16, 16)
            made[pl.ds(place, 16), :] = sums[vec].astype(bf16)
        return carry

    lax.fori_loop(0, rank // 16, part, 0)
    step_rows = 16 * SLOTS

    def some(step, carry):
        start = pl.multiple_of(step * step_rows, step_rows)
        send_ref[pl.ds(start, step_rows), :] = nt(
            one_hot(step_rows, dest - start), made[...]
        ).astype(bf16)
        return carry

    lax.fori_loop(0, peers * SLOTS // step_rows, some, 0)


def upper(peers, rank, ups, up_t, up_c):
    offset, number = 0, peers
    device = lax.axis_index("leaf")

    def at(node):
        return pl.ds(pl.multiple_of(node * 8, 8), 8)

    gains = []
    while number > 1:
        node = device // (peers // number)
        sibling = node + 1 - 2 * (node % 2)
        partner = ups[at(offset + sibling), :rank]
        gains.append((offset + node, wide(nn, partner, up_c[offset + node])))
        if number > 2:

            def pair(parent, carry, offset=offset, number=number):
                total = 0.0
                for side in range(2):
                    child = offset + 2 * parent + side
                    total = total + wide(nn, ups[at(child), :rank], up_t[child])
                ups[at(offset + number + parent), :] = twice(total)
                return carry

            lax.fori_loop(0, number // 2, pair, 0, unroll=min(8, number // 2))
        offset += number
        number //= 2
    top = gains[-1][1]
    for node, gain in reversed(gains[:-1]):
        top = wide(nt, top, up_t[node]) + gain
    return top


def near_features(mine, other, vx, fa, fb, cols):
    mine = mine.astype(f32)
    other = other.astype(f32)
    vx[:, cols] = jnp.concatenate([mine[:8], other[:8]], axis=0).astype(bf16)
    place = mine[8:]
    square = place[0:1] * place[0:1] + place[1:2] * place[1:2]
    square = square + place[2:3] * place[2:3] + smooth_sq / 2
    high = square.astype(bf16).astype(f32)
    middle = (square - high).astype(bf16).astype(f32)
    low = square - high - middle
    row = lax.broadcasted_iota(i32, place.shape, 0)
    one = jnp.ones_like(place)
    first = jnp.where(row == 3, high, jnp.where(row == 4, middle, jnp.where(row == 5, low, one)))
    first = jnp.where(row < 3, -2.0 * place, first)
    second = jnp.where(row < 6, one, jnp.where(row == 6, high, middle))
    second = jnp.where(row < 3, place, second)
    last = row == 0
    fa[:, cols] = jnp.concatenate([first, jnp.where(last, one, 0.0)], axis=0).astype(bf16)
    fb[:, cols] = jnp.concatenate([second, jnp.where(last, low, 0.0)], axis=0).astype(bf16)


def near_leaf(vx, fa, fb, acc, leaf_len, leaf):
    tgt = leaf_columns(leaf, leaf_len)
    targets = fa[:, tgt]
    total = None
    for step in range(-NEAR, NEAR + 1):
        src = leaf_columns(leaf + step, leaf_len)
        kernel = lax.rsqrt(tn(targets, fb[:, src]).astype(bf16))
        part = nt(kernel, vx[:, src])
        total = part if total is None else total + part
    unit = lax.broadcasted_iota(i32, (ROWS, ROWS), 0) == lax.broadcasted_iota(
        i32, (ROWS, ROWS), 1
    )
    unit = jnp.where(unit, 1.0, 0.0).astype(bf16)
    high = total.astype(bf16)
    low = (total - high.astype(f32)).astype(bf16)
    acc[:, tgt] = nt(unit, high) + nt(unit, low)


def finish(
    top_value, sums, near_all, trans_ref, bases_ref, perm_ref, out_ref, coupled, down, total
):
    leaf_dev, rank, leaf_len = bases_ref.shape
    cols = perm_ref.shape[1]
    groups = cols // WIDTH
    for vec in range(8):
        coupled[pl.ds(vec, SLOTS, stride=8), :] = twice(sums[:, vec * rank : (vec + 1) * rank])
    top = (2 * leaf_dev - 2) * 8
    down[top : top + 8, :] = top_value + coupled[top : top + 8, :rank]
    number = 1
    while number < leaf_dev:
        above = 2 * leaf_dev - 2 * number
        number *= 2
        offset = 2 * leaf_dev - 2 * number
        for child in range(number):
            parent = (above + child // 2) * 8
            place = (offset + child) * 8
            down[place : place + 8, :] = (
                wide(nt, down[parent : parent + 8, :], trans_ref[offset + child])
                + coupled[place : place + 8, :rank]
            )
    total[...] = jnp.zeros_like(total)

    def one_leaf(leaf, carry):
        here = leaf_columns(leaf, leaf_len)
        perm = perm_ref[:, here]
        high = lax.shift_right_logical(perm, SHIFT)
        value = down[pl.ds(pl.multiple_of(leaf * 8, 8), 8), :].astype(bf16)
        tree = nn(value, bases_ref[leaf]) + near_all[:, here] * (near_scale / leaf_len)
        tree = tree.astype(bf16).astype(f32)
        masked = jnp.concatenate(
            [jnp.where(high == group, tree, 0.0) for group in range(groups)], axis=0
        ).astype(bf16)
        total[...] += nt(masked, one_hot(WIDTH, perm & (WIDTH - 1)))
        return carry

    lax.fori_loop(0, leaf_dev, one_leaf, 0, unroll=4)
    for group in range(groups):
        out_ref[:, group * WIDTH : (group + 1) * WIDTH] = total[
            group * 8 : (group + 1) * 8, :
        ].astype(bf16)


def remote(source, target, send_sem, recv_sem, leaf, vec):
    return pltpu.make_async_remote_copy(
        src_ref=source,
        dst_ref=target,
        send_sem=send_sem,
        recv_sem=recv_sem,
        device_id=(leaf, vec),
        device_id_type=pl.DeviceIdType.MESH,
    )


def whole_kernel(
    peers, leaf_len, vec_any, pts_any, perm_any, src_any, owner_any, target_any,
    bases_any, trans_any, blocks_any, up_t_any, up_c_any, out_ref,
    vec_ref, pts_ref, perm_ref, src_ref, owner_ref, target_ref, bases, trans, blocks, up_t, up_c, both, stack, coeff, picked, made, send, recv, roots, ups,
    mine, other, halo, vx, fa, fb, acc, near_all, coupled, down, total,
    local_sem, part_sem, halo_send, halo_recv, root_send, root_recv, block_send, block_recv,
):
    cols = vec_any.shape[1]
    leaf_dev = cols // leaf_len
    rank = trans_any.shape[1]
    reach = NEAR * leaf_len
    half = leaf_dev // 2
    device = lax.axis_index("leaf")
    core = lax.axis_index("vec")
    partner = 1 - core
    cross = device - 1 + 2 * core
    has_cross = jnp.logical_and(cross >= 0, cross < peers)
    barrier = pltpu.get_barrier_semaphore()

    def greet(leaf, vec):
        pl.semaphore_signal(
            barrier, inc=1, device_id=(leaf, vec), device_id_type=pl.DeviceIdType.MESH
        )

    def each_peer(work):
        def body(step, carry):
            work(lax.rem(device + step, peers))
            return carry

        lax.fori_loop(1, peers, body, 0)

    each_peer(lambda peer: greet(peer, core))
    greet(device, partner)

    @pl.when(has_cross)
    def _():
        greet(cross, partner)

    loads = [
        pltpu.make_async_copy(source, target, local_sem.at[place])
        for place, (source, target) in enumerate(
            [(perm_any, perm_ref), (vec_any, vec_ref), (pts_any, pts_ref), (bases_any, bases),
             (trans_any, trans), (src_any, src_ref), (blocks_any, blocks),
             (owner_any, owner_ref), (target_any, target_ref), (up_t_any, up_t),
             (up_c_any, up_c)]
        )
    ]
    for load in loads:
        load.start()
    for load in loads[:4]:
        load.wait()
    to_tree(vec_ref, pts_ref, perm_ref, bases, mine, 0, both, stack, coeff)
    pl.semaphore_wait(barrier, peers + jnp.where(has_cross, 1, 0))

    seen = (half + NEAR) * leaf_len
    shift = (half - NEAR) * leaf_len
    to_partner = remote(
        mine.at[:, pl.ds(pl.multiple_of(partner * shift, 128), seen)], other,
        part_sem.at[0], part_sem.at[1], device, partner,
    )
    to_partner.start()
    to_right = remote(
        mine.at[:, cols - reach :], halo.at[core], halo_send.at[0], halo_recv.at[core],
        device + 1, 0,
    )
    to_left = remote(
        mine.at[:, :reach], halo.at[core], halo_send.at[1], halo_recv.at[core], device - 1, 1
    )
    not_last = device < peers - 1
    not_first = device > 0

    @pl.when(not_last)
    def _():
        to_right.start()

    @pl.when(not_first)
    def _():
        to_left.start()

    loads[4].wait()
    climb(leaf_dev, rank, trans, coeff)
    top = (2 * leaf_dev - 2) * 8
    mine_rows = pl.ds(pl.multiple_of(device * 8, 8), 8)
    ups[mine_rows, :] = coeff[top : top + 8, :]

    def root_copy(peer, place):
        return remote(
            coeff.at[top : top + 8, :], roots.at[place], root_send.at[peer],
            root_recv.at[place], peer, core,
        )

    each_peer(lambda peer: root_copy(peer, device).start())
    for load in loads[5:9]:
        load.wait()
    dest = owner_ref[...] * SLOTS + target_ref[...]
    couple(peers, blocks, src_ref, dest, coeff, picked, made, send)

    def slot(place):
        return pl.ds(pl.multiple_of(place * SLOTS, SLOTS), SLOTS)

    def block_copy(peer, place):
        return remote(
            send.at[slot(peer), :], recv.at[slot(place), :], block_send.at[peer],
            block_recv.at[place], peer, core,
        )

    each_peer(lambda peer: block_copy(peer, device).start())

    to_partner.wait_recv()
    off = NEAR * (1 - core)

    def features(place, carry):
        here = leaf_columns(place, leaf_len)
        there = leaf_columns(place + core * (half - NEAR), leaf_len)
        near_features(
            mine[:, there], other[:, here], vx, fa, fb, leaf_columns(place + off, leaf_len)
        )
        return carry

    lax.fori_loop(0, half + NEAR, features, 0)

    @pl.when(has_cross)
    def _():
        for vec in range(2):
            remote(
                mine.at[:, :reach], halo.at[vec], halo_send.at[vec], halo_recv.at[vec],
                device, partner,
            ).wait_recv()

    @pl.when(jnp.logical_not(has_cross))
    def _():
        halo[...] = jnp.zeros_like(halo)

    for place in range(NEAR):
        here = slice(place * leaf_len, (place + 1) * leaf_len)
        near_features(
            halo[core, :, here], halo[partner, :, here], vx, fa, fb,
            leaf_columns(place + core * (half + NEAR), leaf_len),
        )

    def body(leaf, carry):
        near_leaf(vx, fa, fb, acc, leaf_len, leaf)
        return carry

    lax.fori_loop(NEAR, half + NEAR, body, 0)
    part = half * leaf_len
    computed = pl.ds(pl.multiple_of(core * part, 128), part)
    to_near = remote(
        acc.at[8:16, pl.ds(reach, part)], near_all.at[:, computed],
        part_sem.at[2], part_sem.at[3], device, partner,
    )
    to_near.start()
    near_all[:, computed] = acc[:8, reach : reach + part]

    loads[9].wait()
    loads[10].wait()

    def root_in(peer):
        root_copy(peer, peer).wait_recv()
        ups[pl.ds(pl.multiple_of(peer * 8, 8), 8), :] = roots[peer]

    each_peer(root_in)
    top_value = upper(peers, rank, ups, up_t, up_c)

    def add(step, value):
        peer = lax.rem(device + step, peers)
        block_copy(peer, peer).wait_recv()
        return value + recv[slot(peer), :].astype(f32)

    sums = lax.fori_loop(1, peers, add, send[slot(device), :].astype(f32))
    to_near.wait_recv()
    finish(top_value, sums, near_all, trans, bases, perm_ref, out_ref, coupled, down, total)

    to_partner.wait_send()
    to_near.wait_send()

    @pl.when(not_last)
    def _():
        to_right.wait_send()

    @pl.when(not_first)
    def _():
        to_left.wait_send()

    def sent(peer):
        root_copy(peer, device).wait_send()
        block_copy(peer, device).wait_send()

    each_peer(sent)


def shards(
    points, vectors, leaf_order, leaf_bases, transfers, coupling_blocks,
    block_source, block_owner, block_target, up_transfer, up_coupling,
):
    peers = lax.axis_size("leaf")
    leaf_dev, rank, leaf_len = leaf_bases.shape
    cols = vectors.shape[1]
    blocks = coupling_blocks.shape[0]
    reach = NEAR * leaf_len
    groups = cols // WIDTH
    half = leaf_dev // 2
    span = (half + 2 * NEAR) * leaf_len
    by_block = jnp.transpose(coupling_blocks, (1, 2, 0))
    vmem = pl.BlockSpec(memory_space=pltpu.VMEM)
    anywhere = pl.BlockSpec(memory_space=pl.ANY)
    dma = pltpu.SemaphoreType.DMA
    return pl.pallas_call(
        functools.partial(whole_kernel, peers, leaf_len),
        out_shape=jax.ShapeDtypeStruct((8, cols), bf16),
        in_specs=[anywhere] * 11,
        out_specs=vmem,
        scratch_shapes=[
            pltpu.VMEM(vectors.shape, bf16),
            pltpu.VMEM(points.shape, bf16),
            pltpu.VMEM(leaf_order.shape, i32),
            pltpu.VMEM((1, blocks), i32),
            pltpu.VMEM((1, blocks), i32),
            pltpu.VMEM((1, blocks), i32),
            pltpu.VMEM(leaf_bases.shape, bf16),
            pltpu.VMEM(transfers.shape, bf16),
            pltpu.VMEM(by_block.shape, bf16),
            pltpu.VMEM(up_transfer.shape, bf16),
            pltpu.VMEM(up_coupling.shape, bf16),
            pltpu.VMEM((ROWS, cols), f32),
            pltpu.VMEM((groups * ROWS, WIDTH), bf16),
            pltpu.VMEM((SLOTS * 8, 2 * rank), f32),
            pltpu.VMEM((8 * rank, blocks), f32),
            pltpu.VMEM((8 * rank, blocks), bf16),
            pltpu.VMEM((peers * SLOTS, 8 * rank), bf16),
            pltpu.VMEM((peers * SLOTS, 8 * rank), bf16),
            pltpu.VMEM((peers, 8, 2 * rank), f32),
            pltpu.VMEM((2 * peers * 8, 2 * rank), f32),
            pltpu.VMEM((ROWS, cols), bf16),
            pltpu.VMEM((ROWS, (half + NEAR) * leaf_len), bf16),
            pltpu.VMEM((2, ROWS, reach), bf16),
            pltpu.VMEM((ROWS, span), bf16),
            pltpu.VMEM((ROWS, span), bf16),
            pltpu.VMEM((ROWS, span), bf16),
            pltpu.VMEM((ROWS, span), f32),
            pltpu.VMEM((8, cols), f32),
            pltpu.VMEM((SLOTS * 8, 2 * rank), f32),
            pltpu.VMEM((SLOTS * 8, rank), f32),
            pltpu.VMEM((groups * 8, WIDTH), f32),
            dma((11,)),
            dma((4,)),
            dma((2,)),
            dma((2,)),
            dma((peers,)),
            dma((peers,)),
            dma((peers,)),
            dma((peers,)),
        ],
        compiler_params=pltpu.CompilerParams(
            vmem_limit_bytes=64 * 1024 * 1024, collective_id=0, has_side_effects=True
        ),
        name="whole",
    )(
        vectors, points, leaf_order,
        block_source.reshape(1, blocks), block_owner.reshape(1, blocks),
        block_target.reshape(1, blocks),
        leaf_bases, transfers, by_block, up_transfer, up_coupling,
    )


def solution(mesh):
    return jax.shard_map(
        shards,
        mesh=mesh,
        in_specs=(
            P(None, "leaf"),
            P("vec", "leaf"),
            P("leaf", None),
            P("leaf", None, None),
            P("leaf", None, None),
            P("leaf", None, None),
            P("leaf"),
            P("leaf", None),
            P("leaf"),
            P(),
            P(),
        ),
        out_specs=P("vec", "leaf"),
        check_vma=False,
    )
```

```python
import functools

import jax
import jax.numpy as jnp
from jax import lax
from jax.experimental import pallas as pl
from jax.experimental.pallas import tpu as pltpu
from jax.sharding import PartitionSpec as P

NEAR = 2
WIDTH = 256
SHIFT = 8
ROWS = 16
SLOTS = 32
near_scale = 8.0
smooth_sq = 0.0025
f32, bf16, i32 = jnp.float32, jnp.bfloat16, jnp.int32


def contract(left, right, dim_left, dim_right):
    return lax.dot_general(
        left, right, (((dim_left,), (dim_right,)), ((), ())), preferred_element_type=f32
    )


def nn(left, right):
    return contract(left, right, 1, 0)


def nt(left, right):
    return contract(left, right, 1, 1)


def tn(left, right):
    return contract(left, right, 0, 0)


def two_parts(value):
    high = value.astype(bf16).astype(f32)
    return jnp.concatenate([high, value - high], axis=0).astype(bf16)


def wide(product, value, matrix):
    count = value.shape[0]
    both = product(two_parts(value), matrix)
    return both[:count] + both[count:]


def one_hot(rows, index):
    ids = lax.broadcasted_iota(i32, (rows, index.shape[1]), 0)
    return jnp.where(ids == index, 1.0, 0.0).astype(bf16)


def twice(value):
    return jnp.concatenate([value, value], axis=1)


def leaf_columns(leaf, leaf_len):
    return pl.ds(pl.multiple_of(leaf * leaf_len, leaf_len), leaf_len)


def to_tree(vec_ref, pts_ref, perm_ref, bases_ref, tree_ref, tree_base, both, stack, coeff):
    local, cols = vec_ref.shape
    leaf_dev, rank, leaf_len = bases_ref.shape
    groups = cols // WIDTH
    both[...] = jnp.zeros_like(both)
    both[0:local] = vec_ref[...].astype(f32)
    both[8:11] = pts_ref[...].astype(f32)
    for group in range(groups):
        stack[group * ROWS : (group + 1) * ROWS, :] = both[
            :, group * WIDTH : (group + 1) * WIDTH
        ].astype(bf16)

    def one_leaf(leaf, carry):
        perm = perm_ref[:, leaf_columns(leaf, leaf_len)]
        high = lax.shift_right_logical(perm, SHIFT)
        parts = []
        for part in range(leaf_len // WIDTH):
            here = slice(part * WIDTH, (part + 1) * WIDTH)
            high_part = high[:, here]
            hot = one_hot(WIDTH, perm[:, here] & (WIDTH - 1))
            total = None
            for first in range(0, groups, ROWS):
                picked = nn(stack[first * ROWS : (first + ROWS) * ROWS, :], hot)
                for group in range(ROWS):
                    chosen = jnp.where(
                        high_part == first + group, picked[group * ROWS : (group + 1) * ROWS], 0.0
                    )
                    total = chosen if total is None else total + chosen
            parts.append(total)
        tree = jnp.concatenate(parts, axis=1).astype(bf16)
        tree_ref[:, leaf_columns(leaf + tree_base, leaf_len)] = tree
        own = nt(tree, bases_ref[leaf])[:local]
        coeff[pl.ds(pl.multiple_of(leaf * 8, 8), 8), :] = twice(own)
        return carry

    lax.fori_loop(0, leaf_dev, one_leaf, 0, unroll=4)


def climb(leaf_dev, rank, trans_ref, coeff):
    clusters = 2 * leaf_dev - 1
    coeff[clusters * 8 :, :] = jnp.zeros((coeff.shape[0] - clusters * 8, 2 * rank), f32)
    offset, number = 0, leaf_dev
    while number > 1:
        for parent in range(number // 2):
            total = 0.0
            for child in (offset + 2 * parent, offset + 2 * parent + 1):
                value = coeff[child * 8 : child * 8 + 8, :rank]
                total = total + wide(nn, value, trans_ref[child])
            place = (offset + number + parent) * 8
            coeff[place : place + 8, :] = twice(total)
        offset += number
        number //= 2


def couple(peers, blocks_ref, src_ref, dest, coeff, picked, made, send_ref):
    rank, _, blocks = blocks_ref.shape
    hot = one_hot(SLOTS, src_ref[...])
    for vec in range(8):
        values = coeff[pl.ds(vec, SLOTS, stride=8), :].astype(bf16)
        picked[vec * rank : (vec + 1) * rank, :] = tn(values, hot)[:rank]

    def part(block, carry):
        rows = pl.ds(pl.multiple_of(block * 16, 16), 16)

        def eight(step, sums):
            for inner in range(8):
                place = step * 8 + inner
                matrix = blocks_ref[place, rows, :].astype(f32)
                sums = tuple(
                    value + matrix * picked[pl.ds(vec * rank + place, 1), :]
                    for vec, value in enumerate(sums)
                )
            return sums

        zero = jnp.zeros((16, blocks), f32)
        sums = lax.fori_loop(0, rank // 8, eight, (zero,) * 8)
        for vec in range(8):
            place = pl.multiple_of(vec * rank + block * 16, 16)
            made[pl.ds(place, 16), :] = sums[vec].astype(bf16)
        return carry

    lax.fori_loop(0, rank // 16, part, 0)
    step_rows = 16 * SLOTS

    def some(step, carry):
        start = pl.multiple_of(step * step_rows, step_rows)
        send_ref[pl.ds(start, step_rows), :] = nt(
            one_hot(step_rows, dest - start), made[...]
        ).astype(bf16)
        return carry

    lax.fori_loop(0, peers * SLOTS // step_rows, some, 0)


def upper(peers, rank, ups, up_t, up_c):
    offset, number = 0, peers
    device = lax.axis_index("leaf")

    def at(node):
        return pl.ds(pl.multiple_of(node * 8, 8), 8)

    gains = []
    while number > 1:
        node = device // (peers // number)
        sibling = node + 1 - 2 * (node % 2)
        partner = ups[at(offset + sibling), :rank]
        gains.append((offset + node, wide(nn, partner, up_c[offset + node])))
        if number > 2:

            def pair(parent, carry, offset=offset, number=number):
                total = 0.0
                for side in range(2):
                    child = offset + 2 * parent + side
                    total = total + wide(nn, ups[at(child), :rank], up_t[child])
                ups[at(offset + number + parent), :] = twice(total)
                return carry

            lax.fori_loop(0, number // 2, pair, 0, unroll=min(8, number // 2))
        offset += number
        number //= 2
    top = gains[-1][1]
    for node, gain in reversed(gains[:-1]):
        top = wide(nt, top, up_t[node]) + gain
    return top


def near_features(mine, other, vx, far, fb, cols):
    mine = mine.astype(f32)
    other = other.astype(f32)
    vx[:, cols] = jnp.concatenate([mine[:8], other[:8]], axis=0).astype(bf16)
    place = mine[8:]
    square = place[0:1] * place[0:1] + place[1:2] * place[1:2]
    square = square + place[2:3] * place[2:3] + smooth_sq / 2
    high = square.astype(bf16).astype(f32)
    middle = (square - high).astype(bf16).astype(f32)
    low = square - high - middle
    row = lax.broadcasted_iota(i32, place.shape, 0)
    one = jnp.ones_like(place)
    first = jnp.where(row == 3, high, jnp.where(row == 4, middle, jnp.where(row == 5, low, one)))
    first = jnp.where(row < 3, -2.0 * place, first)
    second = jnp.where(row < 6, one, jnp.where(row == 6, high, middle))
    second = jnp.where(row < 3, place, second)
    last = row == 0
    first = jnp.concatenate([first, jnp.where(last, one, 0.0)], axis=0).astype(bf16)
    unit = lax.broadcasted_iota(i32, (ROWS, ROWS), 0)
    unit = jnp.where(unit == lax.broadcasted_iota(i32, (ROWS, ROWS), 1), 1.0, 0.0).astype(bf16)
    far[cols, :] = tn(first, unit).astype(bf16)
    fb[:, cols] = jnp.concatenate([second, jnp.where(last, low, 0.0)], axis=0).astype(bf16)


def near_source(vx, far, fb, acc, leaf_len, leaf, steps, back):
    parts = leaf_len // WIDTH
    sums = {}

    def columns(step, part):
        return pl.ds(pl.multiple_of((leaf + step) * leaf_len + part * WIDTH, WIDTH), WIDTH)

    def add(key, value):
        sums[key] = sums[key] + value if key in sums else value

    for step in steps:
        for tgt_part in range(parts):
            for src_part in range(parts):
                if step == 0 and src_part > tgt_part:
                    continue
                src, tgt = columns(0, src_part), columns(step, tgt_part)
                square = nn(far[src, :], fb[:, tgt])
                kernel = lax.rsqrt(square.astype(bf16))
                add((step, tgt_part), nn(vx[:, src], kernel))
                if back and (step, tgt_part) != (0, src_part):
                    add((0, src_part), nt(vx[:, tgt], kernel))
    for (step, part), value in sums.items():
        acc[:, columns(step, part)] += value


def finish(
    top_value, sums, near_all, trans_ref, bases_ref, perm_ref, out_ref, coupled, down, total
):
    leaf_dev, rank, leaf_len = bases_ref.shape
    cols = perm_ref.shape[1]
    groups = cols // WIDTH
    for vec in range(8):
        coupled[pl.ds(vec, SLOTS, stride=8), :] = twice(sums[:, vec * rank : (vec + 1) * rank])
    top = (2 * leaf_dev - 2) * 8
    down[top : top + 8, :] = top_value + coupled[top : top + 8, :rank]
    number = 1
    while number < leaf_dev:
        above = 2 * leaf_dev - 2 * number
        number *= 2
        offset = 2 * leaf_dev - 2 * number
        for child in range(number):
            parent = (above + child // 2) * 8
            place = (offset + child) * 8
            down[place : place + 8, :] = (
                wide(nt, down[parent : parent + 8, :], trans_ref[offset + child])
                + coupled[place : place + 8, :rank]
            )
    total[...] = jnp.zeros_like(total)

    def one_leaf(leaf, carry):
        here = leaf_columns(leaf, leaf_len)
        perm = perm_ref[:, here]
        high = lax.shift_right_logical(perm, SHIFT)
        value = down[pl.ds(pl.multiple_of(leaf * 8, 8), 8), :].astype(bf16)
        tree = nn(value, bases_ref[leaf]) + near_all[:, here] * (near_scale / leaf_len)
        tree = tree.astype(bf16).astype(f32)
        masked = jnp.concatenate(
            [jnp.where(high == group, tree, 0.0) for group in range(groups)], axis=0
        ).astype(bf16)
        total[...] += nt(masked, one_hot(WIDTH, perm & (WIDTH - 1)))
        return carry

    lax.fori_loop(0, leaf_dev, one_leaf, 0, unroll=4)
    for group in range(groups):
        out_ref[:, group * WIDTH : (group + 1) * WIDTH] = total[
            group * 8 : (group + 1) * 8, :
        ].astype(bf16)


def remote(source, target, send_sem, recv_sem, leaf, vec):
    return pltpu.make_async_remote_copy(
        src_ref=source,
        dst_ref=target,
        send_sem=send_sem,
        recv_sem=recv_sem,
        device_id=(leaf, vec),
        device_id_type=pl.DeviceIdType.MESH,
    )


def whole_kernel(
    peers, leaf_len, vec_any, pts_any, perm_any, src_any, owner_any, target_any,
    bases_any, trans_any, blocks_any, up_t_any, up_c_any, out_ref,
    vec_ref, pts_ref, perm_ref, src_ref, owner_ref, target_ref, bases, trans, blocks, up_t, up_c, both, stack, coeff, picked, made, send, recv, roots, ups,
    mine, other, halo, vx, far, fb, acc, near_all, coupled, down, total,
    local_sem, part_sem, halo_send, halo_recv, root_send, root_recv, block_send, block_recv,
):
    cols = vec_any.shape[1]
    leaf_dev = cols // leaf_len
    rank = trans_any.shape[1]
    reach = NEAR * leaf_len
    half = leaf_dev // 2
    device = lax.axis_index("leaf")
    core = lax.axis_index("vec")
    partner = 1 - core
    cross = device - 1 + 2 * core
    has_cross = jnp.logical_and(cross >= 0, cross < peers)
    barrier = pltpu.get_barrier_semaphore()

    def greet(leaf, vec):
        pl.semaphore_signal(
            barrier, inc=1, device_id=(leaf, vec), device_id_type=pl.DeviceIdType.MESH
        )

    def each_peer(work):
        def body(step, carry):
            work(lax.rem(device + step, peers))
            return carry

        lax.fori_loop(1, peers, body, 0)

    each_peer(lambda peer: greet(peer, core))
    greet(device, partner)

    @pl.when(has_cross)
    def _():
        greet(cross, partner)

    loads = [
        pltpu.make_async_copy(source, target, local_sem.at[place])
        for place, (source, target) in enumerate(
            [(perm_any, perm_ref), (vec_any, vec_ref), (pts_any, pts_ref), (bases_any, bases),
             (trans_any, trans), (src_any, src_ref), (blocks_any, blocks),
             (owner_any, owner_ref), (target_any, target_ref), (up_t_any, up_t),
             (up_c_any, up_c)]
        )
    ]
    for load in loads:
        load.start()
    for load in loads[:4]:
        load.wait()
    to_tree(vec_ref, pts_ref, perm_ref, bases, mine, 0, both, stack, coeff)
    pl.semaphore_wait(barrier, peers + jnp.where(has_cross, 1, 0))

    seen = (half + NEAR) * leaf_len
    shift = (half - NEAR) * leaf_len
    to_partner = remote(
        mine.at[:, pl.ds(pl.multiple_of(partner * shift, 128), seen)], other,
        part_sem.at[0], part_sem.at[1], device, partner,
    )
    to_partner.start()
    to_right = remote(
        mine.at[:, cols - reach :], halo.at[core], halo_send.at[0], halo_recv.at[core],
        device + 1, 0,
    )
    to_left = remote(
        mine.at[:, :reach], halo.at[core], halo_send.at[1], halo_recv.at[core], device - 1, 1
    )
    not_last = device < peers - 1
    not_first = device > 0

    @pl.when(not_last)
    def _():
        to_right.start()

    @pl.when(not_first)
    def _():
        to_left.start()

    loads[4].wait()
    climb(leaf_dev, rank, trans, coeff)
    top = (2 * leaf_dev - 2) * 8
    mine_rows = pl.ds(pl.multiple_of(device * 8, 8), 8)
    ups[mine_rows, :] = coeff[top : top + 8, :]

    def root_copy(peer, place):
        return remote(
            coeff.at[top : top + 8, :], roots.at[place], root_send.at[peer],
            root_recv.at[place], peer, core,
        )

    each_peer(lambda peer: root_copy(peer, device).start())
    for load in loads[5:9]:
        load.wait()
    dest = owner_ref[...] * SLOTS + target_ref[...]
    couple(peers, blocks, src_ref, dest, coeff, picked, made, send)

    def slot(place):
        return pl.ds(pl.multiple_of(place * SLOTS, SLOTS), SLOTS)

    def block_copy(peer, place):
        return remote(
            send.at[slot(peer), :], recv.at[slot(place), :], block_send.at[peer],
            block_recv.at[place], peer, core,
        )

    each_peer(lambda peer: block_copy(peer, device).start())

    to_partner.wait_recv()
    off = NEAR * (1 - core)

    def features(place, carry):
        here = leaf_columns(place, leaf_len)
        there = leaf_columns(place + core * (half - NEAR), leaf_len)
        near_features(
            mine[:, there], other[:, here], vx, far, fb, leaf_columns(place + off, leaf_len)
        )
        return carry

    lax.fori_loop(0, half + NEAR, features, 0, unroll=2)

    @pl.when(has_cross)
    def _():
        for vec in range(2):
            remote(
                mine.at[:, :reach], halo.at[vec], halo_send.at[vec], halo_recv.at[vec],
                device, partner,
            ).wait_recv()

    @pl.when(jnp.logical_not(has_cross))
    def _():
        halo[...] = jnp.zeros_like(halo)

    for place in range(NEAR):
        here = slice(place * leaf_len, (place + 1) * leaf_len)
        near_features(
            halo[core, :, here], halo[partner, :, here], vx, far, fb,
            leaf_columns(place + core * (half + NEAR), leaf_len),
        )
    acc[...] = jnp.zeros_like(acc)
    near_source(vx, far, fb, acc, leaf_len, 0, (2,), False)
    near_source(vx, far, fb, acc, leaf_len, 1, (1, 2), False)

    def body(leaf, carry):
        near_source(vx, far, fb, acc, leaf_len, leaf, (0, 1, 2), True)
        return carry

    lax.fori_loop(NEAR, half + NEAR, body, 0)
    part = half * leaf_len
    computed = pl.ds(pl.multiple_of(core * part, 128), part)
    to_near = remote(
        acc.at[8:16, pl.ds(reach, part)], near_all.at[:, computed],
        part_sem.at[2], part_sem.at[3], device, partner,
    )
    to_near.start()
    near_all[:, computed] = acc[:8, reach : reach + part]

    loads[9].wait()
    loads[10].wait()

    def root_in(peer):
        root_copy(peer, peer).wait_recv()
        ups[pl.ds(pl.multiple_of(peer * 8, 8), 8), :] = roots[peer]

    each_peer(root_in)
    top_value = upper(peers, rank, ups, up_t, up_c)

    def add(step, value):
        peer = lax.rem(device + step, peers)
        block_copy(peer, peer).wait_recv()
        return value + recv[slot(peer), :].astype(f32)

    sums = lax.fori_loop(1, peers, add, send[slot(device), :].astype(f32))
    to_near.wait_recv()
    finish(top_value, sums, near_all, trans, bases, perm_ref, out_ref, coupled, down, total)

    to_partner.wait_send()
    to_near.wait_send()

    @pl.when(not_last)
    def _():
        to_right.wait_send()

    @pl.when(not_first)
    def _():
        to_left.wait_send()

    def sent(peer):
        root_copy(peer, device).wait_send()
        block_copy(peer, device).wait_send()

    each_peer(sent)


def shards(
    points, vectors, leaf_order, leaf_bases, transfers, coupling_blocks,
    block_source, block_owner, block_target, up_transfer, up_coupling,
):
    peers = lax.axis_size("leaf")
    leaf_dev, rank, leaf_len = leaf_bases.shape
    cols = vectors.shape[1]
    blocks = coupling_blocks.shape[0]
    reach = NEAR * leaf_len
    groups = cols // WIDTH
    half = leaf_dev // 2
    span = (half + 2 * NEAR) * leaf_len
    by_block = jnp.transpose(coupling_blocks, (1, 2, 0))
    vmem = pl.BlockSpec(memory_space=pltpu.VMEM)
    anywhere = pl.BlockSpec(memory_space=pl.ANY)
    dma = pltpu.SemaphoreType.DMA
    return pl.pallas_call(
        functools.partial(whole_kernel, peers, leaf_len),
        out_shape=jax.ShapeDtypeStruct((8, cols), bf16),
        in_specs=[anywhere] * 11,
        out_specs=vmem,
        scratch_shapes=[
            pltpu.VMEM(vectors.shape, bf16),
            pltpu.VMEM(points.shape, bf16),
            pltpu.VMEM(leaf_order.shape, i32),
            pltpu.VMEM((1, blocks), i32),
            pltpu.VMEM((1, blocks), i32),
            pltpu.VMEM((1, blocks), i32),
            pltpu.VMEM(leaf_bases.shape, bf16),
            pltpu.VMEM(transfers.shape, bf16),
            pltpu.VMEM(by_block.shape, bf16),
            pltpu.VMEM(up_transfer.shape, bf16),
            pltpu.VMEM(up_coupling.shape, bf16),
            pltpu.VMEM((ROWS, cols), f32),
            pltpu.VMEM((groups * ROWS, WIDTH), bf16),
            pltpu.VMEM((SLOTS * 8, 2 * rank), f32),
            pltpu.VMEM((8 * rank, blocks), f32),
            pltpu.VMEM((8 * rank, blocks), bf16),
            pltpu.VMEM((peers * SLOTS, 8 * rank), bf16),
            pltpu.VMEM((peers * SLOTS, 8 * rank), bf16),
            pltpu.VMEM((peers, 8, 2 * rank), f32),
            pltpu.VMEM((2 * peers * 8, 2 * rank), f32),
            pltpu.VMEM((ROWS, cols), bf16),
            pltpu.VMEM((ROWS, (half + NEAR) * leaf_len), bf16),
            pltpu.VMEM((2, ROWS, reach), bf16),
            pltpu.VMEM((ROWS, span), bf16),
            pltpu.VMEM((span, ROWS), bf16),
            pltpu.VMEM((ROWS, span), bf16),
            pltpu.VMEM((ROWS, span), f32),
            pltpu.VMEM((8, cols), f32),
            pltpu.VMEM((SLOTS * 8, 2 * rank), f32),
            pltpu.VMEM((SLOTS * 8, rank), f32),
            pltpu.VMEM((groups * 8, WIDTH), f32),
            dma((11,)),
            dma((4,)),
            dma((2,)),
            dma((2,)),
            dma((peers,)),
            dma((peers,)),
            dma((peers,)),
            dma((peers,)),
        ],
        compiler_params=pltpu.CompilerParams(
            vmem_limit_bytes=64 * 1024 * 1024, collective_id=0, has_side_effects=True
        ),
        name="whole",
    )(
        vectors, points, leaf_order,
        block_source.reshape(1, blocks), block_owner.reshape(1, blocks),
        block_target.reshape(1, blocks),
        leaf_bases, transfers, by_block, up_transfer, up_coupling,
    )


def solution(mesh):
    return jax.shard_map(
        shards,
        mesh=mesh,
        in_specs=(
            P(None, "leaf"),
            P("vec", "leaf"),
            P("leaf", None),
            P("leaf", None, None),
            P("leaf", None, None),
            P("leaf", None, None),
            P("leaf"),
            P("leaf", None),
            P("leaf"),
            P(),
            P(),
        ),
        out_specs=P("vec", "leaf"),
        check_vma=False,
    )
```

```python
import functools
import math

import jax
import jax.numpy as jnp
from jax import lax
from jax.experimental import pallas as pl
from jax.experimental.pallas import tpu as pltpu
from jax.sharding import PartitionSpec as P

NEAR = 2
WIDTH = 256
SHIFT = 8
ROWS = 16
SLOTS = 32
near_scale = 8.0
smooth_sq = 0.0025
half_log = -0.5 / math.log(2.0)
f32, bf16, i32 = jnp.float32, jnp.bfloat16, jnp.int32


def contract(left, right, dim_left, dim_right):
    return lax.dot_general(
        left, right, (((dim_left,), (dim_right,)), ((), ())), preferred_element_type=f32
    )


def nn(left, right):
    return contract(left, right, 1, 0)


def nt(left, right):
    return contract(left, right, 1, 1)


def tn(left, right):
    return contract(left, right, 0, 0)


def two_parts(value):
    high = value.astype(bf16).astype(f32)
    return jnp.concatenate([high, value - high], axis=0).astype(bf16)


def wide(product, value, matrix):
    count = value.shape[0]
    both = product(two_parts(value), matrix)
    return both[:count] + both[count:]


def one_hot(rows, index):
    ids = lax.broadcasted_iota(i32, (rows, index.shape[1]), 0)
    return jnp.where(ids == index, 1.0, 0.0).astype(bf16)


def twice(value):
    return jnp.concatenate([value, value], axis=1)


def leaf_columns(leaf, leaf_len):
    return pl.ds(pl.multiple_of(leaf * leaf_len, leaf_len), leaf_len)


def to_tree(vec_ref, pts_ref, perm_ref, bases_ref, tree_ref, tree_base, both, stack, coeff):
    local, cols = vec_ref.shape
    leaf_dev, rank, leaf_len = bases_ref.shape
    groups = cols // WIDTH
    both[...] = jnp.zeros_like(both)
    both[0:local] = vec_ref[...].astype(f32)
    both[8:11] = pts_ref[...].astype(f32)
    for group in range(groups):
        stack[group * ROWS : (group + 1) * ROWS, :] = both[
            :, group * WIDTH : (group + 1) * WIDTH
        ].astype(bf16)

    def one_leaf(leaf, carry):
        perm = perm_ref[:, leaf_columns(leaf, leaf_len)]
        high = lax.shift_right_logical(perm, SHIFT)
        picked = nn(stack[...], one_hot(WIDTH, perm & (WIDTH - 1)))
        total = jnp.where(high == 0, picked[:ROWS], 0.0)
        for group in range(1, groups):
            total = total + jnp.where(
                high == group, picked[group * ROWS : (group + 1) * ROWS], 0.0
            )
        tree = total.astype(bf16)
        tree_ref[:, leaf_columns(leaf + tree_base, leaf_len)] = tree
        own = nt(tree, bases_ref[leaf])[:local]
        coeff[pl.ds(pl.multiple_of(leaf * 8, 8), 8), :] = twice(own)
        return carry

    lax.fori_loop(0, leaf_dev, one_leaf, 0, unroll=4)


def climb(leaf_dev, rank, trans_ref, coeff):
    clusters = 2 * leaf_dev - 1
    coeff[clusters * 8 :, :] = jnp.zeros((coeff.shape[0] - clusters * 8, 2 * rank), f32)
    offset, number = 0, leaf_dev
    while number > 1:
        for parent in range(number // 2):
            total = 0.0
            for child in (offset + 2 * parent, offset + 2 * parent + 1):
                value = coeff[child * 8 : child * 8 + 8, :rank]
                total = total + wide(nn, value, trans_ref[child])
            place = (offset + number + parent) * 8
            coeff[place : place + 8, :] = twice(total)
        offset += number
        number //= 2


def couple(peers, blocks_ref, src_ref, dest, coeff, picked, made, send_ref):
    rank, _, blocks = blocks_ref.shape
    hot = one_hot(SLOTS, src_ref[...])
    for vec in range(8):
        values = coeff[pl.ds(vec, SLOTS, stride=8), :].astype(bf16)
        picked[vec * rank : (vec + 1) * rank, :] = tn(values, hot)[:rank]

    def part(block, carry):
        rows = pl.ds(pl.multiple_of(block * 16, 16), 16)

        def eight(step, sums):
            for inner in range(8):
                place = step * 8 + inner
                matrix = blocks_ref[place, rows, :].astype(f32)
                sums = tuple(
                    value + matrix * picked[pl.ds(vec * rank + place, 1), :]
                    for vec, value in enumerate(sums)
                )
            return sums

        zero = jnp.zeros((16, blocks), f32)
        sums = lax.fori_loop(0, rank // 8, eight, (zero,) * 8)
        for vec in range(8):
            place = pl.multiple_of(vec * rank + block * 16, 16)
            made[pl.ds(place, 16), :] = sums[vec].astype(bf16)
        return carry

    lax.fori_loop(0, rank // 16, part, 0)
    step_rows = 16 * SLOTS

    def some(step, carry):
        start = pl.multiple_of(step * step_rows, step_rows)
        send_ref[pl.ds(start, step_rows), :] = nt(
            one_hot(step_rows, dest - start), made[...]
        ).astype(bf16)
        return carry

    lax.fori_loop(0, peers * SLOTS // step_rows, some, 0)


def upper(peers, rank, ups, up_t, up_c):
    offset, number = 0, peers
    device = lax.axis_index("leaf")

    def at(node):
        return pl.ds(pl.multiple_of(node * 8, 8), 8)

    gains = []
    while number > 1:
        node = device // (peers // number)
        sibling = node + 1 - 2 * (node % 2)
        partner = ups[at(offset + sibling), :rank]
        gains.append((offset + node, wide(nn, partner, up_c[offset + node])))
        if number > 2:

            def pair(parent, carry, offset=offset, number=number):
                total = 0.0
                for side in range(2):
                    child = offset + 2 * parent + side
                    total = total + wide(nn, ups[at(child), :rank], up_t[child])
                ups[at(offset + number + parent), :] = twice(total)
                return carry

            lax.fori_loop(0, number // 2, pair, 0, unroll=min(8, number // 2))
        offset += number
        number //= 2
    top = gains[-1][1]
    for node, gain in reversed(gains[:-1]):
        top = wide(nt, top, up_t[node]) + gain
    return top


def near_features(mine, other, vx, fa, fb, cols):
    mine = mine.astype(f32)
    other = other.astype(f32)
    vx[:, cols] = jnp.concatenate([mine[:8], other[:8]], axis=0).astype(bf16)
    place = mine[8:]
    square = place[0:1] * place[0:1] + place[1:2] * place[1:2]
    square = square + place[2:3] * place[2:3] + smooth_sq / 2
    high = square.astype(bf16).astype(f32)
    middle = (square - high).astype(bf16).astype(f32)
    low = square - high - middle
    row = lax.broadcasted_iota(i32, place.shape, 0)
    one = jnp.ones_like(place)
    first = jnp.where(row == 3, high, jnp.where(row == 4, middle, jnp.where(row == 5, low, one)))
    first = jnp.where(row < 3, -2.0 * place, first)
    second = jnp.where(row < 6, one, jnp.where(row == 6, high, middle))
    second = jnp.where(row < 3, place, second)
    last = row == 0
    fa[:, cols] = jnp.concatenate([first, jnp.where(last, one, 0.0)], axis=0).astype(bf16)
    fb[:, cols] = jnp.concatenate([second, jnp.where(last, low, 0.0)], axis=0).astype(bf16)


def near_pairs(ext, fa, fb, acc, leaf_len, source, targets, back):
    src = leaf_columns(source, leaf_len)
    for target in targets:
        tgt = leaf_columns(target, leaf_len)
        kernel = jnp.exp2(lax.log(tn(fa[:, src], fb[:, tgt])) * half_log).astype(bf16)
        acc[:, tgt] += nn(ext[:, src], kernel)
        if back and target is not source:
            acc[:, src] += nt(ext[:, tgt], kernel)


def finish(
    top_value, sums, near_all, trans_ref, bases_ref, perm_ref, out_ref, coupled, down, total
):
    leaf_dev, rank, leaf_len = bases_ref.shape
    cols = perm_ref.shape[1]
    groups = cols // WIDTH
    for vec in range(8):
        coupled[pl.ds(vec, SLOTS, stride=8), :] = twice(sums[:, vec * rank : (vec + 1) * rank])
    top = (2 * leaf_dev - 2) * 8
    down[top : top + 8, :] = top_value + coupled[top : top + 8, :rank]
    number = 1
    while number < leaf_dev:
        above = 2 * leaf_dev - 2 * number
        number *= 2
        offset = 2 * leaf_dev - 2 * number
        for child in range(number):
            parent = (above + child // 2) * 8
            place = (offset + child) * 8
            down[place : place + 8, :] = (
                wide(nt, down[parent : parent + 8, :], trans_ref[offset + child])
                + coupled[place : place + 8, :rank]
            )
    total[...] = jnp.zeros_like(total)

    def one_leaf(leaf, carry):
        here = leaf_columns(leaf, leaf_len)
        perm = perm_ref[:, here]
        high = lax.shift_right_logical(perm, SHIFT)
        value = down[pl.ds(pl.multiple_of(leaf * 8, 8), 8), :].astype(bf16)
        tree = nn(value, bases_ref[leaf]) + near_all[:, here] * (near_scale / leaf_len)
        tree = tree.astype(bf16).astype(f32)
        masked = jnp.concatenate(
            [jnp.where(high == group, tree, 0.0) for group in range(groups)], axis=0
        ).astype(bf16)
        total[...] += nt(masked, one_hot(WIDTH, perm & (WIDTH - 1)))
        return carry

    lax.fori_loop(0, leaf_dev, one_leaf, 0, unroll=4)
    for group in range(groups):
        out_ref[:, group * WIDTH : (group + 1) * WIDTH] = total[
            group * 8 : (group + 1) * 8, :
        ].astype(bf16)


def remote(source, target, send_sem, recv_sem, leaf, vec):
    return pltpu.make_async_remote_copy(
        src_ref=source,
        dst_ref=target,
        send_sem=send_sem,
        recv_sem=recv_sem,
        device_id=(leaf, vec),
        device_id_type=pl.DeviceIdType.MESH,
    )


def whole_kernel(
    peers, leaf_len, vec_any, pts_any, perm_any, src_any, owner_any, target_any,
    bases_any, trans_any, blocks_any, up_t_any, up_c_any, out_ref,
    vec_ref, pts_ref, perm_ref, src_ref, owner_ref, target_ref, bases, trans, blocks, up_t, up_c, both, stack, coeff, picked, made, send, recv, roots, ups,
    mine, other, halo, vx, fa, fb, acc, near_all, coupled, down, total,
    local_sem, part_sem, halo_send, halo_recv, root_send, root_recv, block_send, block_recv,
):
    cols = vec_any.shape[1]
    leaf_dev = cols // leaf_len
    rank = trans_any.shape[1]
    reach = NEAR * leaf_len
    half = leaf_dev // 2
    device = lax.axis_index("leaf")
    core = lax.axis_index("vec")
    partner = 1 - core
    cross = device - 1 + 2 * core
    has_cross = jnp.logical_and(cross >= 0, cross < peers)
    barrier = pltpu.get_barrier_semaphore()

    def greet(leaf, vec):
        pl.semaphore_signal(
            barrier, inc=1, device_id=(leaf, vec), device_id_type=pl.DeviceIdType.MESH
        )

    def each_peer(work):
        def body(step, carry):
            work(lax.rem(device + step, peers))
            return carry

        lax.fori_loop(1, peers, body, 0)

    each_peer(lambda peer: greet(peer, core))
    greet(device, partner)

    @pl.when(has_cross)
    def _():
        greet(cross, partner)

    loads = [
        pltpu.make_async_copy(source, target, local_sem.at[place])
        for place, (source, target) in enumerate(
            [(perm_any, perm_ref), (vec_any, vec_ref), (pts_any, pts_ref), (bases_any, bases),
             (trans_any, trans), (src_any, src_ref), (blocks_any, blocks),
             (owner_any, owner_ref), (target_any, target_ref), (up_t_any, up_t),
             (up_c_any, up_c)]
        )
    ]
    for load in loads:
        load.start()
    for load in loads[:4]:
        load.wait()
    to_tree(vec_ref, pts_ref, perm_ref, bases, mine, 0, both, stack, coeff)
    pl.semaphore_wait(barrier, peers + jnp.where(has_cross, 1, 0))

    seen = (half + NEAR) * leaf_len
    shift = (half - NEAR) * leaf_len
    to_partner = remote(
        mine.at[:, pl.ds(pl.multiple_of(partner * shift, 128), seen)], other,
        part_sem.at[0], part_sem.at[1], device, partner,
    )
    to_partner.start()
    to_right = remote(
        mine.at[:, cols - reach :], halo.at[core], halo_send.at[0], halo_recv.at[core],
        device + 1, 0,
    )
    to_left = remote(
        mine.at[:, :reach], halo.at[core], halo_send.at[1], halo_recv.at[core], device - 1, 1
    )
    not_last = device < peers - 1
    not_first = device > 0

    @pl.when(not_last)
    def _():
        to_right.start()

    @pl.when(not_first)
    def _():
        to_left.start()

    loads[4].wait()
    climb(leaf_dev, rank, trans, coeff)
    top = (2 * leaf_dev - 2) * 8
    mine_rows = pl.ds(pl.multiple_of(device * 8, 8), 8)
    ups[mine_rows, :] = coeff[top : top + 8, :]

    def root_copy(peer, place):
        return remote(
            coeff.at[top : top + 8, :], roots.at[place], root_send.at[peer],
            root_recv.at[place], peer, core,
        )

    each_peer(lambda peer: root_copy(peer, device).start())
    for load in loads[5:9]:
        load.wait()
    dest = owner_ref[...] * SLOTS + target_ref[...]
    couple(peers, blocks, src_ref, dest, coeff, picked, made, send)

    def slot(place):
        return pl.ds(pl.multiple_of(place * SLOTS, SLOTS), SLOTS)

    def block_copy(peer, place):
        return remote(
            send.at[slot(peer), :], recv.at[slot(place), :], block_send.at[peer],
            block_recv.at[place], peer, core,
        )

    each_peer(lambda peer: block_copy(peer, device).start())

    to_partner.wait_recv()
    off = NEAR * (1 - core)

    def features(place, carry):
        here = leaf_columns(place, leaf_len)
        there = leaf_columns(place + core * (half - NEAR), leaf_len)
        near_features(
            mine[:, there], other[:, here], vx, fa, fb, leaf_columns(place + off, leaf_len)
        )
        return carry

    lax.fori_loop(0, half + NEAR, features, 0)

    @pl.when(has_cross)
    def _():
        for vec in range(2):
            remote(
                mine.at[:, :reach], halo.at[vec], halo_send.at[vec], halo_recv.at[vec],
                device, partner,
            ).wait_recv()

    @pl.when(jnp.logical_not(has_cross))
    def _():
        halo[...] = jnp.zeros_like(halo)

    for place in range(NEAR):
        here = slice(place * leaf_len, (place + 1) * leaf_len)
        near_features(
            halo[core, :, here], halo[partner, :, here], vx, fa, fb,
            leaf_columns(place + core * (half + NEAR), leaf_len),
        )
    acc[...] = jnp.zeros_like(acc)
    near_pairs(vx, fa, fb, acc, leaf_len, 0, (2,), False)
    near_pairs(vx, fa, fb, acc, leaf_len, 1, (2, 3), False)

    def body(leaf, carry):
        near_pairs(vx, fa, fb, acc, leaf_len, leaf, (leaf, leaf + 1, leaf + 2), True)
        return carry

    lax.fori_loop(NEAR, half + NEAR, body, 0)
    part = half * leaf_len
    computed = pl.ds(pl.multiple_of(core * part, 128), part)
    to_near = remote(
        acc.at[8:16, pl.ds(reach, part)], near_all.at[:, computed],
        part_sem.at[2], part_sem.at[3], device, partner,
    )
    to_near.start()
    near_all[:, computed] = acc[:8, reach : reach + part]

    loads[9].wait()
    loads[10].wait()

    def root_in(peer):
        root_copy(peer, peer).wait_recv()
        ups[pl.ds(pl.multiple_of(peer * 8, 8), 8), :] = roots[peer]

    each_peer(root_in)
    top_value = upper(peers, rank, ups, up_t, up_c)

    def add(step, value):
        peer = lax.rem(device + step, peers)
        block_copy(peer, peer).wait_recv()
        return value + recv[slot(peer), :].astype(f32)

    sums = lax.fori_loop(1, peers, add, send[slot(device), :].astype(f32))
    to_near.wait_recv()
    finish(top_value, sums, near_all, trans, bases, perm_ref, out_ref, coupled, down, total)

    to_partner.wait_send()
    to_near.wait_send()

    @pl.when(not_last)
    def _():
        to_right.wait_send()

    @pl.when(not_first)
    def _():
        to_left.wait_send()

    def sent(peer):
        root_copy(peer, device).wait_send()
        block_copy(peer, device).wait_send()

    each_peer(sent)


def shards(
    points, vectors, leaf_order, leaf_bases, transfers, coupling_blocks,
    block_source, block_owner, block_target, up_transfer, up_coupling,
):
    peers = lax.axis_size("leaf")
    leaf_dev, rank, leaf_len = leaf_bases.shape
    cols = vectors.shape[1]
    blocks = coupling_blocks.shape[0]
    reach = NEAR * leaf_len
    groups = cols // WIDTH
    half = leaf_dev // 2
    span = (half + 2 * NEAR) * leaf_len
    by_block = jnp.transpose(coupling_blocks, (1, 2, 0))
    vmem = pl.BlockSpec(memory_space=pltpu.VMEM)
    anywhere = pl.BlockSpec(memory_space=pl.ANY)
    dma = pltpu.SemaphoreType.DMA
    return pl.pallas_call(
        functools.partial(whole_kernel, peers, leaf_len),
        out_shape=jax.ShapeDtypeStruct((8, cols), bf16),
        in_specs=[anywhere] * 11,
        out_specs=vmem,
        scratch_shapes=[
            pltpu.VMEM(vectors.shape, bf16),
            pltpu.VMEM(points.shape, bf16),
            pltpu.VMEM(leaf_order.shape, i32),
            pltpu.VMEM((1, blocks), i32),
            pltpu.VMEM((1, blocks), i32),
            pltpu.VMEM((1, blocks), i32),
            pltpu.VMEM(leaf_bases.shape, bf16),
            pltpu.VMEM(transfers.shape, bf16),
            pltpu.VMEM(by_block.shape, bf16),
            pltpu.VMEM(up_transfer.shape, bf16),
            pltpu.VMEM(up_coupling.shape, bf16),
            pltpu.VMEM((ROWS, cols), f32),
            pltpu.VMEM((groups * ROWS, WIDTH), bf16),
            pltpu.VMEM((SLOTS * 8, 2 * rank), f32),
            pltpu.VMEM((8 * rank, blocks), f32),
            pltpu.VMEM((8 * rank, blocks), bf16),
            pltpu.VMEM((peers * SLOTS, 8 * rank), bf16),
            pltpu.VMEM((peers * SLOTS, 8 * rank), bf16),
            pltpu.VMEM((peers, 8, 2 * rank), f32),
            pltpu.VMEM((2 * peers * 8, 2 * rank), f32),
            pltpu.VMEM((ROWS, cols), bf16),
            pltpu.VMEM((ROWS, (half + NEAR) * leaf_len), bf16),
            pltpu.VMEM((2, ROWS, reach), bf16),
            pltpu.VMEM((ROWS, span), bf16),
            pltpu.VMEM((ROWS, span), bf16),
            pltpu.VMEM((ROWS, span), bf16),
            pltpu.VMEM((ROWS, span), f32),
            pltpu.VMEM((8, cols), f32),
            pltpu.VMEM((SLOTS * 8, 2 * rank), f32),
            pltpu.VMEM((SLOTS * 8, rank), f32),
            pltpu.VMEM((groups * 8, WIDTH), f32),
            dma((11,)),
            dma((4,)),
            dma((2,)),
            dma((2,)),
            dma((peers,)),
            dma((peers,)),
            dma((peers,)),
            dma((peers,)),
        ],
        compiler_params=pltpu.CompilerParams(
            vmem_limit_bytes=64 * 1024 * 1024, collective_id=0, has_side_effects=True
        ),
        name="whole",
    )(
        vectors, points, leaf_order,
        block_source.reshape(1, blocks), block_owner.reshape(1, blocks),
        block_target.reshape(1, blocks),
        leaf_bases, transfers, by_block, up_transfer, up_coupling,
    )


def solution(mesh):
    return jax.shard_map(
        shards,
        mesh=mesh,
        in_specs=(
            P(None, "leaf"),
            P("vec", "leaf"),
            P("leaf", None),
            P("leaf", None, None),
            P("leaf", None, None),
            P("leaf", None, None),
            P("leaf"),
            P("leaf", None),
            P("leaf"),
            P(),
            P(),
        ),
        out_specs=P("vec", "leaf"),
        check_vma=False,
    )
```

```python
import functools

import jax
import jax.numpy as jnp
from jax import lax
from jax.experimental import pallas as pl
from jax.experimental.pallas import tpu as pltpu
from jax.sharding import PartitionSpec as P

NEAR = 2
WIDTH = 256
SHIFT = 8
ROWS = 16
SLOTS = 32
near_scale = 8.0
smooth_sq = 0.0025
f32, bf16, i32 = jnp.float32, jnp.bfloat16, jnp.int32


def contract(left, right, dim_left, dim_right):
    return lax.dot_general(
        left, right, (((dim_left,), (dim_right,)), ((), ())), preferred_element_type=f32
    )


def nn(left, right):
    return contract(left, right, 1, 0)


def nt(left, right):
    return contract(left, right, 1, 1)


def tn(left, right):
    return contract(left, right, 0, 0)


def two_parts(value):
    high = value.astype(bf16).astype(f32)
    return jnp.concatenate([high, value - high], axis=0).astype(bf16)


def wide(product, value, matrix):
    count = value.shape[0]
    both = product(two_parts(value), matrix)
    return both[:count] + both[count:]


def one_hot(rows, index):
    ids = lax.broadcasted_iota(i32, (rows, index.shape[1]), 0)
    return jnp.where(ids == index, 1.0, 0.0).astype(bf16)


def twice(value):
    return jnp.concatenate([value, value], axis=1)


def leaf_columns(leaf, leaf_len):
    return pl.ds(pl.multiple_of(leaf * leaf_len, leaf_len), leaf_len)


def to_tree(vec_ref, pts_ref, perm_ref, bases_ref, tree_ref, tree_base, both, stack, coeff):
    local, cols = vec_ref.shape
    leaf_dev, rank, leaf_len = bases_ref.shape
    groups = cols // WIDTH
    both[...] = jnp.zeros_like(both)
    both[0:local] = vec_ref[...].astype(f32)
    both[8:11] = pts_ref[...].astype(f32)
    for group in range(groups):
        stack[group * ROWS : (group + 1) * ROWS, :] = both[
            :, group * WIDTH : (group + 1) * WIDTH
        ].astype(bf16)

    def one_leaf(leaf, carry):
        perm = perm_ref[:, leaf_columns(leaf, leaf_len)]
        high = lax.shift_right_logical(perm, SHIFT)
        picked = nn(stack[...], one_hot(WIDTH, perm & (WIDTH - 1)))
        total = jnp.where(high == 0, picked[:ROWS], 0.0)
        for group in range(1, groups):
            total = total + jnp.where(
                high == group, picked[group * ROWS : (group + 1) * ROWS], 0.0
            )
        tree = total.astype(bf16)
        tree_ref[:, leaf_columns(leaf + tree_base, leaf_len)] = tree
        own = nt(tree, bases_ref[leaf])[:local]
        coeff[pl.ds(pl.multiple_of(leaf * 8, 8), 8), :] = twice(own)
        return carry

    lax.fori_loop(0, leaf_dev, one_leaf, 0, unroll=4)


def climb(leaf_dev, rank, trans_ref, coeff):
    clusters = 2 * leaf_dev - 1
    coeff[clusters * 8 :, :] = jnp.zeros((coeff.shape[0] - clusters * 8, 2 * rank), f32)
    offset, number = 0, leaf_dev
    while number > 1:
        for parent in range(number // 2):
            total = 0.0
            for child in (offset + 2 * parent, offset + 2 * parent + 1):
                value = coeff[child * 8 : child * 8 + 8, :rank]
                total = total + wide(nn, value, trans_ref[child])
            place = (offset + number + parent) * 8
            coeff[place : place + 8, :] = twice(total)
        offset += number
        number //= 2


def couple(peers, blocks_ref, src_ref, dest, coeff, picked, made, send_ref):
    rank, _, blocks = blocks_ref.shape
    hot = one_hot(SLOTS, src_ref[...])
    for vec in range(8):
        values = coeff[pl.ds(vec, SLOTS, stride=8), :].astype(bf16)
        picked[vec * rank : (vec + 1) * rank, :] = tn(values, hot)[:rank]

    def part(block, carry):
        rows = pl.ds(pl.multiple_of(block * 16, 16), 16)

        def eight(step, sums):
            for inner in range(8):
                place = step * 8 + inner
                matrix = blocks_ref[place, rows, :].astype(f32)
                sums = tuple(
                    value + matrix * picked[pl.ds(vec * rank + place, 1), :]
                    for vec, value in enumerate(sums)
                )
            return sums

        zero = jnp.zeros((16, blocks), f32)
        sums = lax.fori_loop(0, rank // 8, eight, (zero,) * 8)
        for vec in range(8):
            place = pl.multiple_of(vec * rank + block * 16, 16)
            made[pl.ds(place, 16), :] = sums[vec].astype(bf16)
        return carry

    lax.fori_loop(0, rank // 16, part, 0)
    step_rows = 16 * SLOTS

    def some(step, carry):
        start = pl.multiple_of(step * step_rows, step_rows)
        send_ref[pl.ds(start, step_rows), :] = nt(
            one_hot(step_rows, dest - start), made[...]
        ).astype(bf16)
        return carry

    lax.fori_loop(0, peers * SLOTS // step_rows, some, 0)


def upper(peers, rank, ups, up_t, up_c):
    offset, number = 0, peers
    device = lax.axis_index("leaf")

    def at(node):
        return pl.ds(pl.multiple_of(node * 8, 8), 8)

    gains = []
    while number > 1:
        node = device // (peers // number)
        sibling = node + 1 - 2 * (node % 2)
        partner = ups[at(offset + sibling), :rank]
        gains.append((offset + node, wide(nn, partner, up_c[offset + node])))
        if number > 2:

            def pair(parent, carry, offset=offset, number=number):
                total = 0.0
                for side in range(2):
                    child = offset + 2 * parent + side
                    total = total + wide(nn, ups[at(child), :rank], up_t[child])
                ups[at(offset + number + parent), :] = twice(total)
                return carry

            lax.fori_loop(0, number // 2, pair, 0, unroll=min(8, number // 2))
        offset += number
        number //= 2
    top = gains[-1][1]
    for node, gain in reversed(gains[:-1]):
        top = wide(nt, top, up_t[node]) + gain
    return top


def near_features(mine, other, vx, fa, fb, cols):
    mine = mine.astype(f32)
    other = other.astype(f32)
    vx[:, cols] = jnp.concatenate([mine[:8], other[:8]], axis=0).astype(bf16)
    place = mine[8:]
    square = place[0:1] * place[0:1] + place[1:2] * place[1:2]
    square = square + place[2:3] * place[2:3] + smooth_sq / 2
    high = square.astype(bf16).astype(f32)
    middle = (square - high).astype(bf16).astype(f32)
    low = square - high - middle
    row = lax.broadcasted_iota(i32, place.shape, 0)
    one = jnp.ones_like(place)
    first = jnp.where(row == 3, high, jnp.where(row == 4, middle, jnp.where(row == 5, low, one)))
    first = jnp.where(row < 3, -2.0 * place, first)
    second = jnp.where(row < 6, one, jnp.where(row == 6, high, middle))
    second = jnp.where(row < 3, place, second)
    last = row == 0
    fa[:, cols] = jnp.concatenate([first, jnp.where(last, one, 0.0)], axis=0).astype(bf16)
    fb[:, cols] = jnp.concatenate([second, jnp.where(last, low, 0.0)], axis=0).astype(bf16)


def near_pairs(ext, fa, fb, acc, leaf_len, source, targets, back):
    src = leaf_columns(source, leaf_len)
    own = None
    for target in targets:
        tgt = leaf_columns(target, leaf_len)
        kernel = lax.rsqrt(tn(fa[:, src], fb[:, tgt])).astype(bf16)
        forward = nn(ext[:, src], kernel)
        if target is source:
            own = forward
        else:
            acc[:, tgt] += forward
            if back:
                own = own + nt(ext[:, tgt], kernel)
    if back:
        acc[:, src] += own


def finish(
    top_value, sums, near_all, trans_ref, bases_ref, perm_ref, out_ref, coupled, down, total
):
    leaf_dev, rank, leaf_len = bases_ref.shape
    cols = perm_ref.shape[1]
    groups = cols // WIDTH
    for vec in range(8):
        coupled[pl.ds(vec, SLOTS, stride=8), :] = twice(sums[:, vec * rank : (vec + 1) * rank])
    top = (2 * leaf_dev - 2) * 8
    down[top : top + 8, :] = top_value + coupled[top : top + 8, :rank]
    number = 1
    while number < leaf_dev:
        above = 2 * leaf_dev - 2 * number
        number *= 2
        offset = 2 * leaf_dev - 2 * number
        for child in range(number):
            parent = (above + child // 2) * 8
            place = (offset + child) * 8
            down[place : place + 8, :] = (
                wide(nt, down[parent : parent + 8, :], trans_ref[offset + child])
                + coupled[place : place + 8, :rank]
            )
    total[...] = jnp.zeros_like(total)

    def one_leaf(leaf, carry):
        here = leaf_columns(leaf, leaf_len)
        perm = perm_ref[:, here]
        high = lax.shift_right_logical(perm, SHIFT)
        value = down[pl.ds(pl.multiple_of(leaf * 8, 8), 8), :].astype(bf16)
        tree = nn(value, bases_ref[leaf]) + near_all[:, here] * (near_scale / leaf_len)
        tree = tree.astype(bf16).astype(f32)
        masked = jnp.concatenate(
            [jnp.where(high == group, tree, 0.0) for group in range(groups)], axis=0
        ).astype(bf16)
        total[...] += nt(masked, one_hot(WIDTH, perm & (WIDTH - 1)))
        return carry

    lax.fori_loop(0, leaf_dev, one_leaf, 0, unroll=4)
    for group in range(groups):
        out_ref[:, group * WIDTH : (group + 1) * WIDTH] = total[
            group * 8 : (group + 1) * 8, :
        ].astype(bf16)


def remote(source, target, send_sem, recv_sem, leaf, vec):
    return pltpu.make_async_remote_copy(
        src_ref=source,
        dst_ref=target,
        send_sem=send_sem,
        recv_sem=recv_sem,
        device_id=(leaf, vec),
        device_id_type=pl.DeviceIdType.MESH,
    )


def whole_kernel(
    peers, leaf_len, vec_any, pts_any, perm_any, src_any, owner_any, target_any,
    bases_any, trans_any, blocks_any, up_t_any, up_c_any, out_ref,
    vec_ref, pts_ref, perm_ref, src_ref, owner_ref, target_ref, bases, trans, blocks, up_t, up_c, both, stack, coeff, picked, made, send, recv, roots, ups,
    mine, other, halo, vx, fa, fb, acc, near_all, coupled, down, total,
    local_sem, part_sem, halo_send, halo_recv, root_send, root_recv, block_send, block_recv,
):
    cols = vec_any.shape[1]
    leaf_dev = cols // leaf_len
    rank = trans_any.shape[1]
    reach = NEAR * leaf_len
    half = leaf_dev // 2
    device = lax.axis_index("leaf")
    core = lax.axis_index("vec")
    partner = 1 - core
    cross = device - 1 + 2 * core
    has_cross = jnp.logical_and(cross >= 0, cross < peers)
    barrier = pltpu.get_barrier_semaphore()

    def greet(leaf, vec):
        pl.semaphore_signal(
            barrier, inc=1, device_id=(leaf, vec), device_id_type=pl.DeviceIdType.MESH
        )

    def each_peer(work):
        def body(step, carry):
            work(lax.rem(device + step, peers))
            return carry

        lax.fori_loop(1, peers, body, 0)

    each_peer(lambda peer: greet(peer, core))
    greet(device, partner)

    @pl.when(has_cross)
    def _():
        greet(cross, partner)

    loads = [
        pltpu.make_async_copy(source, target, local_sem.at[place])
        for place, (source, target) in enumerate(
            [(perm_any, perm_ref), (vec_any, vec_ref), (pts_any, pts_ref), (bases_any, bases),
             (trans_any, trans), (src_any, src_ref), (blocks_any, blocks),
             (owner_any, owner_ref), (target_any, target_ref), (up_t_any, up_t),
             (up_c_any, up_c)]
        )
    ]
    for load in loads:
        load.start()
    for load in loads[:4]:
        load.wait()
    to_tree(vec_ref, pts_ref, perm_ref, bases, mine, 0, both, stack, coeff)
    pl.semaphore_wait(barrier, peers + jnp.where(has_cross, 1, 0))

    seen = (half + NEAR) * leaf_len
    shift = (half - NEAR) * leaf_len
    to_partner = remote(
        mine.at[:, pl.ds(pl.multiple_of(partner * shift, 128), seen)], other,
        part_sem.at[0], part_sem.at[1], device, partner,
    )
    to_partner.start()
    to_right = remote(
        mine.at[:, cols - reach :], halo.at[core], halo_send.at[0], halo_recv.at[core],
        device + 1, 0,
    )
    to_left = remote(
        mine.at[:, :reach], halo.at[core], halo_send.at[1], halo_recv.at[core], device - 1, 1
    )
    not_last = device < peers - 1
    not_first = device > 0

    @pl.when(not_last)
    def _():
        to_right.start()

    @pl.when(not_first)
    def _():
        to_left.start()

    loads[4].wait()
    climb(leaf_dev, rank, trans, coeff)
    top = (2 * leaf_dev - 2) * 8
    mine_rows = pl.ds(pl.multiple_of(device * 8, 8), 8)
    ups[mine_rows, :] = coeff[top : top + 8, :]

    def root_copy(peer, place):
        return remote(
            coeff.at[top : top + 8, :], roots.at[place], root_send.at[peer],
            root_recv.at[place], peer, core,
        )

    each_peer(lambda peer: root_copy(peer, device).start())
    for load in loads[5:9]:
        load.wait()
    dest = owner_ref[...] * SLOTS + target_ref[...]
    couple(peers, blocks, src_ref, dest, coeff, picked, made, send)

    def slot(place):
        return pl.ds(pl.multiple_of(place * SLOTS, SLOTS), SLOTS)

    def block_copy(peer, place):
        return remote(
            send.at[slot(peer), :], recv.at[slot(place), :], block_send.at[peer],
            block_recv.at[place], peer, core,
        )

    each_peer(lambda peer: block_copy(peer, device).start())

    to_partner.wait_recv()
    off = NEAR * (1 - core)

    def features(place, carry):
        here = leaf_columns(place, leaf_len)
        there = leaf_columns(place + core * (half - NEAR), leaf_len)
        near_features(
            mine[:, there], other[:, here], vx, fa, fb, leaf_columns(place + off, leaf_len)
        )
        return carry

    lax.fori_loop(0, half + NEAR, features, 0)

    @pl.when(has_cross)
    def _():
        for vec in range(2):
            remote(
                mine.at[:, :reach], halo.at[vec], halo_send.at[vec], halo_recv.at[vec],
                device, partner,
            ).wait_recv()

    @pl.when(jnp.logical_not(has_cross))
    def _():
        halo[...] = jnp.zeros_like(halo)

    for place in range(NEAR):
        here = slice(place * leaf_len, (place + 1) * leaf_len)
        near_features(
            halo[core, :, here], halo[partner, :, here], vx, fa, fb,
            leaf_columns(place + core * (half + NEAR), leaf_len),
        )
    acc[...] = jnp.zeros_like(acc)
    near_pairs(vx, fa, fb, acc, leaf_len, 0, (2,), False)
    near_pairs(vx, fa, fb, acc, leaf_len, 1, (2, 3), False)

    def body(leaf, carry):
        near_pairs(vx, fa, fb, acc, leaf_len, leaf, (leaf, leaf + 1, leaf + 2), True)
        return carry

    lax.fori_loop(NEAR, half + NEAR, body, 0, unroll=2)
    part = half * leaf_len
    computed = pl.ds(pl.multiple_of(core * part, 128), part)
    to_near = remote(
        acc.at[8:16, pl.ds(reach, part)], near_all.at[:, computed],
        part_sem.at[2], part_sem.at[3], device, partner,
    )
    to_near.start()
    near_all[:, computed] = acc[:8, reach : reach + part]

    loads[9].wait()
    loads[10].wait()

    def root_in(peer):
        root_copy(peer, peer).wait_recv()
        ups[pl.ds(pl.multiple_of(peer * 8, 8), 8), :] = roots[peer]

    each_peer(root_in)
    top_value = upper(peers, rank, ups, up_t, up_c)

    def add(step, value):
        peer = lax.rem(device + step, peers)
        block_copy(peer, peer).wait_recv()
        return value + recv[slot(peer), :].astype(f32)

    sums = lax.fori_loop(1, peers, add, send[slot(device), :].astype(f32))
    to_near.wait_recv()
    finish(top_value, sums, near_all, trans, bases, perm_ref, out_ref, coupled, down, total)

    to_partner.wait_send()
    to_near.wait_send()

    @pl.when(not_last)
    def _():
        to_right.wait_send()

    @pl.when(not_first)
    def _():
        to_left.wait_send()

    def sent(peer):
        root_copy(peer, device).wait_send()
        block_copy(peer, device).wait_send()

    each_peer(sent)


def shards(
    points, vectors, leaf_order, leaf_bases, transfers, coupling_blocks,
    block_source, block_owner, block_target, up_transfer, up_coupling,
):
    peers = lax.axis_size("leaf")
    leaf_dev, rank, leaf_len = leaf_bases.shape
    cols = vectors.shape[1]
    blocks = coupling_blocks.shape[0]
    reach = NEAR * leaf_len
    groups = cols // WIDTH
    half = leaf_dev // 2
    span = (half + 2 * NEAR) * leaf_len
    by_block = jnp.transpose(coupling_blocks, (1, 2, 0))
    vmem = pl.BlockSpec(memory_space=pltpu.VMEM)
    anywhere = pl.BlockSpec(memory_space=pl.ANY)
    dma = pltpu.SemaphoreType.DMA
    return pl.pallas_call(
        functools.partial(whole_kernel, peers, leaf_len),
        out_shape=jax.ShapeDtypeStruct((8, cols), bf16),
        in_specs=[anywhere] * 11,
        out_specs=vmem,
        scratch_shapes=[
            pltpu.VMEM(vectors.shape, bf16),
            pltpu.VMEM(points.shape, bf16),
            pltpu.VMEM(leaf_order.shape, i32),
            pltpu.VMEM((1, blocks), i32),
            pltpu.VMEM((1, blocks), i32),
            pltpu.VMEM((1, blocks), i32),
            pltpu.VMEM(leaf_bases.shape, bf16),
            pltpu.VMEM(transfers.shape, bf16),
            pltpu.VMEM(by_block.shape, bf16),
            pltpu.VMEM(up_transfer.shape, bf16),
            pltpu.VMEM(up_coupling.shape, bf16),
            pltpu.VMEM((ROWS, cols), f32),
            pltpu.VMEM((groups * ROWS, WIDTH), bf16),
            pltpu.VMEM((SLOTS * 8, 2 * rank), f32),
            pltpu.VMEM((8 * rank, blocks), f32),
            pltpu.VMEM((8 * rank, blocks), bf16),
            pltpu.VMEM((peers * SLOTS, 8 * rank), bf16),
            pltpu.VMEM((peers * SLOTS, 8 * rank), bf16),
            pltpu.VMEM((peers, 8, 2 * rank), f32),
            pltpu.VMEM((2 * peers * 8, 2 * rank), f32),
            pltpu.VMEM((ROWS, cols), bf16),
            pltpu.VMEM((ROWS, (half + NEAR) * leaf_len), bf16),
            pltpu.VMEM((2, ROWS, reach), bf16),
            pltpu.VMEM((ROWS, span), bf16),
            pltpu.VMEM((ROWS, span), bf16),
            pltpu.VMEM((ROWS, span), bf16),
            pltpu.VMEM((ROWS, span), f32),
            pltpu.VMEM((8, cols), f32),
            pltpu.VMEM((SLOTS * 8, 2 * rank), f32),
            pltpu.VMEM((SLOTS * 8, rank), f32),
            pltpu.VMEM((groups * 8, WIDTH), f32),
            dma((11,)),
            dma((4,)),
            dma((2,)),
            dma((2,)),
            dma((peers,)),
            dma((peers,)),
            dma((peers,)),
            dma((peers,)),
        ],
        compiler_params=pltpu.CompilerParams(
            vmem_limit_bytes=64 * 1024 * 1024, collective_id=0, has_side_effects=True
        ),
        name="whole",
    )(
        vectors, points, leaf_order,
        block_source.reshape(1, blocks), block_owner.reshape(1, blocks),
        block_target.reshape(1, blocks),
        leaf_bases, transfers, by_block, up_transfer, up_coupling,
    )


def solution(mesh):
    return jax.shard_map(
        shards,
        mesh=mesh,
        in_specs=(
            P(None, "leaf"),
            P("vec", "leaf"),
            P("leaf", None),
            P("leaf", None, None),
            P("leaf", None, None),
            P("leaf", None, None),
            P("leaf"),
            P("leaf", None),
            P("leaf"),
            P(),
            P(),
        ),
        out_specs=P("vec", "leaf"),
        check_vma=False,
    )
```
